32 devices in a mesh: dp: 8 (over y, x, core), ctx: 4 (over z).
Axes of the slice: x: 2, y: 2, z: 4, core: 2. Of those that a mesh axis runs over, the one named last changes fastest.
Arguments:
- inputs: bfloat16 [8192, 2048], P(('dp', 'ctx')), may hold values from -6 to 6
- cotangent: bfloat16 [8192, 2048], P(('dp', 'ctx')), may hold values from -6 to 6
- segment_ids: int32 [8, 1024], P('dp'), may hold values from 0 to 4, as said below
- real_entry_flags: int32 [8, 1024], P('dp'), may hold values from 0 to 1, as said below
- attention_gain: float32 [2048], P(('dp', 'ctx')), may hold values from 0.1 to 1.9
- feedforward_gain: float32 [2048], P(('dp', 'ctx')), may hold values from 0.1 to 1.9
- query_weight: float32 [2048, 2048], P(('dp', 'ctx')), may hold values from -0.125 to 0.125
- key_weight: float32 [2048, 512], P(('dp', 'ctx')), may hold values from -0.125 to 0.125
- value_weight: float32 [2048, 512], P(('dp', 'ctx')), may hold values from -0.125 to 0.125
- output_weight: float32 [2048, 2048], P(('dp', 'ctx')), may hold values from -0.5 to 0.5
- gate_weight: float32 [2048, 8192], P(('dp', 'ctx')), may hold values from -0.125 to 0.125
- up_weight: float32 [2048, 8192], P(('dp', 'ctx')), may hold values from -0.125 to 0.125
- down_weight: float32 [8192, 2048], P(('dp', 'ctx')), may hold values from -0.0625 to 0.0625
Outputs:
- block_output: bfloat16 [8192, 2048], P(('dp', 'ctx'))
- input_grad: bfloat16 [8192, 2048], P(('dp', 'ctx'))
- attention_gain_grad: float32 [2048], P(('dp', 'ctx'))
- feedforward_gain_grad: float32 [2048], P(('dp', 'ctx'))
- query_weight_grad: float32 [2048, 2048], P(('dp', 'ctx'))
- key_weight_grad: float32 [2048, 512], P(('dp', 'ctx'))
- value_weight_grad: float32 [2048, 512], P(('dp', 'ctx'))
- output_weight_grad: float32 [2048, 2048], P(('dp', 'ctx'))
- gate_weight_grad: float32 [2048, 8192], P(('dp', 'ctx'))
- up_weight_grad: float32 [2048, 8192], P(('dp', 'ctx'))
- down_weight_grad: float32 [8192, 2048], P(('dp', 'ctx'))
The draws below stay inside these ranges and needn't reach their ends.
Inputs may be any that keep to these rules, and one draw needn't show every extreme that they name: `segment_ids`: along each sequence the ids never fall and start at 0 or 1; a sequence has at most 5 documents; in every sequence one document begins before position 256 and its last token is at or after position 895. `real_entry_flags`: each row is ones followed by 1 to 64 zeros; the padding tokens carry the id of the sequence's last document.
All inputs are finite; a program needn't handle non-finite values.
Results may differ from the reference program's by a relative error of at most 0.015.
Values may be sent and summed in bfloat16 or wider, within the bound.
No kernel may reach another device: no remote copies, remote signals or barrier semaphores. Data moves between devices by JAX's collectives and lax.ppermute only.
A program may use at most 488 MiB of HBM per device.

```python
import jax
import jax.numpy as jnp
from jax import lax

D = 2048
HEADS = 32
KV_HEADS = 8
HEAD_DIM = 64
FF = 8192
SPAN = 256
SEQS = 8
SEQ_LEN = 1024
TOKENS = 8192


def layout(key):
    key_list = jax.random.split(jax.random.fold_in(key, 17), 4)
    padding = jax.random.randint(key_list[0], (SEQS,), 1, SPAN // 4 + 1)
    genuine_extent = SEQ_LEN - padding
    long_start = jax.random.randint(key_list[1], (SEQS,), 1, SPAN)
    long_end = genuine_extent - jax.random.randint(key_list[2], (SEQS,), 1, SPAN // 4 + 1)
    cut_draws = jax.random.randint(key_list[3], (SEQS, 2), 0, 1 << 20)
    first_cut = cut_draws[:, 0] % long_start
    last_cut = long_end + cut_draws[:, 1] % (genuine_extent - long_end)
    entry_offset = jnp.arange(SEQ_LEN, dtype=jnp.int32)[None, :]
    packed_text_spans = (entry_offset >= first_cut[:, None]).astype(jnp.int32)
    packed_text_spans = packed_text_spans + (entry_offset >= long_start[:, None]).astype(jnp.int32)
    packed_text_spans = packed_text_spans + (entry_offset >= long_end[:, None]).astype(jnp.int32)
    packed_text_spans = packed_text_spans + (entry_offset >= last_cut[:, None]).astype(jnp.int32)
    entry_reality = (entry_offset < genuine_extent[:, None]).astype(jnp.int32)
    return (packed_text_spans, entry_reality)


def draw_segment_ids(key, part):
    return layout(key)[0]


def draw_real_entry_flags(key, part):
    return layout(key)[1]


def block_scale(rng, dims, cuts, smallest, top_value):
    gain, own = 1.0, jax.random.fold_in(rng, 6)
    for position, parts in cuts:
        steps = jnp.exp(jax.random.uniform(jax.random.fold_in(own, position), (parts,), jnp.float32, smallest / len(cuts), top_value / len(cuts)))
        gain = gain * jnp.repeat(steps, dims[position] // parts).reshape([-1 if axis == position else 1 for axis in range(len(dims))])
    return gain


def gaussian(stream_key, shape, scale, reach, cuts=(), kind=jnp.bfloat16):
    values = scale * jax.random.normal(stream_key, shape, jnp.float32)
    if cuts:
        values = values * block_scale(stream_key, shape, cuts, -0.22, 0.18)
    return jnp.clip(values, -reach, reach).astype(kind)


def setup_inputs(seed: int = 0) -> dict:
    splits = jax.random.split(jax.random.key(seed), 14)
    inputs = gaussian(splits[0], (TOKENS, D), 1.0, 6.0, ((0, 32),))
    cotangent = gaussian(splits[1], (TOKENS, D), 1.0, 6.0, ((0, 32),))
    segment_ids = draw_segment_ids(jax.random.fold_in(splits[13], 71), 0)
    real_entry_flags = draw_real_entry_flags(jax.random.fold_in(splits[13], 71), 0)
    attention_gain = jnp.clip(1.0 + 0.18 * jax.random.normal(splits[4], (D,), jnp.float32), 0.1, 1.9)
    feedforward_gain = jnp.clip(1.0 + 0.18 * jax.random.normal(splits[5], (D,), jnp.float32), 0.1, 1.9)
    query_weight = gaussian(splits[6], (D, HEADS * HEAD_DIM), D ** -0.5, 0.125, ((0, 32),), jnp.float32)
    key_weight = gaussian(splits[7], (D, KV_HEADS * HEAD_DIM), D ** -0.5, 0.125, ((0, 32),), jnp.float32)
    value_weight = gaussian(splits[8], (D, KV_HEADS * HEAD_DIM), D ** -0.5, 0.125, ((0, 32),), jnp.float32)
    output_weight = gaussian(splits[9], (HEADS * HEAD_DIM, D), (HEADS * HEAD_DIM // 16) ** -0.5, 0.5, ((0, 32),), jnp.float32)
    gate_weight = gaussian(splits[10], (D, FF), D ** -0.5, 0.125, ((0, 32),), jnp.float32)
    up_weight = gaussian(splits[11], (D, FF), D ** -0.5, 0.125, ((0, 32),), jnp.float32)
    down_weight = gaussian(splits[12], (FF, D), FF ** -0.5, 0.0625, ((0, 32),), jnp.float32)
    return {"inputs": inputs, "cotangent": cotangent, "segment_ids": segment_ids, "real_entry_flags": real_entry_flags, "attention_gain": attention_gain, "feedforward_gain": feedforward_gain, "query_weight": query_weight, "key_weight": key_weight, "value_weight": value_weight, "output_weight": output_weight, "gate_weight": gate_weight, "up_weight": up_weight, "down_weight": down_weight}


@jax.custom_vjp
def low(v):
    return lax.optimization_barrier(v.astype(jnp.bfloat16)).astype(jnp.float32)

@jax.custom_vjp
def low_back(v):
    return v

def low_keep(v):
    return (low(v), None)

def low_pass(kept, grad):
    return (grad,)

def back_keep(v):
    return (v, None)

def back_low(kept, grad):
    return (low(grad),)
low.defvjp(low_keep, low_pass)
low_back.defvjp(back_keep, back_low)
EPSILON = 1e-05
ROPE_BASE = 500000.0
MASKED_SCORE = -1e+30
HIGHEST = lax.Precision.HIGHEST

def product(left, right):
    return jnp.dot(left, right, precision=HIGHEST)

def normed(values):
    return values * lax.rsqrt(lax.optimization_barrier(jnp.mean(values * values, axis=-1, keepdims=True)) + EPSILON)

def turn(values, cosine, sine_table):
    half_dim = values.shape[-1] // 2
    first_half = values[..., :half_dim]
    second_half = values[..., half_dim:]
    return jnp.concatenate([first_half * cosine - second_half * sine_table, second_half * cosine + first_half * sine_table], -1)

def angles(packed_text_spans, opening_entry_index, entry_count, head_dim):
    places = opening_entry_index + jnp.arange(entry_count, dtype=jnp.int32)
    device_span_labels = lax.dynamic_slice_in_dim(packed_text_spans, opening_entry_index, entry_count)
    doc_starts = lax.optimization_barrier(jnp.sum((packed_text_spans[None, :] < device_span_labels[:, None]).astype(jnp.int32), axis=1))
    offsets = (places - doc_starts).astype(jnp.float32)
    half_dim = head_dim // 2
    frequency = ROPE_BASE ** (-(jnp.arange(half_dim, dtype=jnp.float32) * 2.0 / head_dim))
    angle_table = offsets[:, None, None] * frequency[None, None, :]
    return (jnp.cos(angle_table), jnp.sin(angle_table))

def allowed_couplings(packed_text_spans, entry_reality, opening_entry_index, entry_count):
    overall_extent = packed_text_spans.shape[0]
    asking_entry_indices = opening_entry_index + jnp.arange(entry_count, dtype=jnp.int32)
    attended_indices = jnp.arange(overall_extent, dtype=jnp.int32)
    device_span_labels = lax.dynamic_slice_in_dim(packed_text_spans, opening_entry_index, entry_count)
    same_text_span = (device_span_labels[:, None] == packed_text_spans[None, :]) & (attended_indices[None, :] <= asking_entry_indices[:, None]) & (entry_reality[None, :] == 1)
    return same_text_span | (attended_indices[None, :] == asking_entry_indices[:, None])

def apply_single_sample(block_parameters, packed_entries, packed_text_spans, entry_reality):
    gain_first, gain_second, query_w, key_w, value_w, output_w, gate_w, up_w, down_w = block_parameters
    overall_extent = packed_entries.shape[0]
    group_size = HEADS // KV_HEADS
    cosine, sine_table = angles(packed_text_spans, 0, overall_extent, HEAD_DIM)
    causal_allowance = allowed_couplings(packed_text_spans, entry_reality, 0, overall_extent)
    first_hidden = low(normed(packed_entries) * gain_first)
    query_raw = low_back(product(first_hidden, query_w)).reshape(overall_extent, HEADS, HEAD_DIM)
    key_raw = low_back(product(first_hidden, key_w)).reshape(overall_extent, KV_HEADS, HEAD_DIM)
    value_raw = product(first_hidden, value_w).reshape(overall_extent, KV_HEADS, HEAD_DIM)
    queries = low(turn(query_raw, cosine, sine_table)).reshape(overall_extent, KV_HEADS, group_size, HEAD_DIM)
    keys_rot = low(turn(key_raw, cosine, sine_table))
    values_low = low(low_back(value_raw))
    scores = low_back(jnp.einsum('ikgd,jkd->kgij', queries, keys_rot, precision=HIGHEST) * HEAD_DIM ** (-0.5))
    scores = jnp.where(causal_allowance[None, None], scores, MASKED_SCORE)
    row_top = lax.optimization_barrier(jnp.max(scores, axis=-1, keepdims=True))
    exponent = jnp.exp(scores - row_top)
    probs = low(exponent / lax.optimization_barrier(jnp.sum(exponent, axis=-1, keepdims=True)))
    attended = jnp.einsum('kgij,jkd->ikgd', probs, values_low, precision=HIGHEST).reshape(overall_extent, HEADS * HEAD_DIM)
    attended = low(low_back(attended))
    residual = packed_entries + low_back(product(attended, output_w))
    second_hidden = low(normed(residual) * gain_second)
    gate_value = low_back(product(second_hidden, gate_w))
    up_value = low_back(product(second_hidden, up_w))
    active = low(jax.nn.silu(gate_value) * up_value)
    return residual + product(active, down_w)

def reference(inputs, cotangent, segment_ids, real_entry_flags, attention_gain, feedforward_gain, query_weight, key_weight, value_weight, output_weight, gate_weight, up_weight, down_weight):
    masters = (attention_gain, feedforward_gain, query_weight, key_weight, value_weight, output_weight, gate_weight, up_weight, down_weight)

    def forward(packed_entries, params):
        lowered = tuple((low(master) for master in params))
        step_fn = jax.checkpoint(apply_single_sample)

        def one_sequence(carry, item):
            return (carry, step_fn(lowered, item[0], item[1], item[2]))
        _, results = lax.scan(one_sequence, jnp.zeros((), jnp.float32), (packed_entries.reshape(SEQS, SEQ_LEN, D), segment_ids, real_entry_flags))
        return results.reshape(TOKENS, D)
    result, pullback = jax.vjp(forward, inputs.astype(jnp.float32), masters)
    grad_inputs, grads = pullback(cotangent.astype(jnp.float32))
    return (result.astype(jnp.bfloat16), grad_inputs.astype(jnp.bfloat16), grads[0], grads[1], grads[2], grads[3], grads[4], grads[5], grads[6], grads[7], grads[8])
```

```python
import math

import jax
import jax.numpy as jnp
from jax import lax
from jax.sharding import Mesh
from jax.sharding import PartitionSpec as P

HEAD_DIM = 64
EPSILON = 1e-05
ROPE_BASE = 500000.0
MASKED_SCORE = -1e30
LANES = 128

LOW = jnp.bfloat16
WIDE = jnp.float32


def matmul(left, right):
    return jnp.dot(left, right, preferred_element_type=WIDE)


def matmul_left_t(left, right):
    return lax.dot_general(left, right, (((0,), (0,)), ((), ())), preferred_element_type=WIDE)


def matmul_right_t(left, right):
    return lax.dot_general(left, right, (((1,), (1,)), ((), ())), preferred_element_type=WIDE)


def inverse_root(values):
    return lax.rsqrt(jnp.mean(values * values, axis=-1, keepdims=True) + EPSILON)


def norm_back(values, grad_normed):
    scaled = inverse_root(values)
    unit_rows = values * scaled
    return scaled * (
        grad_normed - unit_rows * jnp.mean(grad_normed * unit_rows, axis=-1, keepdims=True)
    )


def turn(values, cosine, sine):
    half_dim = values.shape[-1] // 2
    first_half = values[..., :half_dim]
    second_half = values[..., half_dim:]
    return jnp.concatenate(
        [
            first_half * cosine - second_half * sine,
            second_half * cosine + first_half * sine,
        ],
        -1,
    )


def after(values, *earlier):
    return lax.optimization_barrier((values, *earlier))[0]


def shift(values, count, step, senders):
    pairs = [(i, i + step) for i in senders if 0 <= i + step < count]
    return lax.ppermute(values, "ctx", pairs)


def rotate(values, count, step):
    return lax.ppermute(values, "ctx", [(i, (i + step) % count) for i in range(count)])


def line_gather(own, count, me):
    up, down = [own], [own]
    for s in range(1, count):
        up.append(shift(up[-1], count, 1, range(s - 1, count)))
        down.append(shift(down[-1], count, -1, range(0, count - s + 1)))
    return [own] + [jnp.where(me >= r, up[r], down[count - r]) for r in range(1, count)]


def line_gather_up(own, count):
    slots = [own]
    for s in range(1, count):
        slots.append(shift(slots[-1], count, 1, range(s - 1, count)))
    return slots


def line_scatter(slots, count):
    up = down = None
    for s in range(1, count):
        up_now = slots[s]
        down_now = slots[count - s]
        if up is not None:
            up_now = up_now + up.astype(WIDE)
            down_now = down_now + down.astype(WIDE)
        up = shift(up_now.astype(LOW), count, 1, range(0, s))
        down = shift(down_now.astype(LOW), count, -1, range(count - s, count))
    return slots[0] + up.astype(WIDE) + down.astype(WIDE)


def line_scatter_down(slots, count):
    down = None
    for s in range(1, count):
        down_now = slots[count - s]
        if down is not None:
            down_now = down_now + down.astype(WIDE)
        down = shift(down_now.astype(LOW), count, -1, range(count - s, count))
    return slots[0] + down.astype(WIDE)


def in_order(slots, count, me):
    out = jnp.zeros((count, *slots[0].shape), slots[0].dtype)
    for r in range(count):
        out = lax.dynamic_update_index_in_dim(out, slots[r], lax.rem(me - r + count, count), 0)
    return out


def per_device(
    inputs,
    cotangent,
    segment_ids,
    real_entry_flags,
    attention_gain,
    feedforward_gain,
    query_weight,
    key_weight,
    value_weight,
    output_weight,
    gate_weight,
    up_weight,
    down_weight,
):
    chips = ("y", "x")
    planes = ("y", "x", "core")
    n_ctx = lax.axis_size("ctx")
    n_chips = lax.axis_size(chips)
    n_core = lax.axis_size("core")
    n_dp = n_chips * n_core
    me = lax.axis_index("ctx")
    core = lax.axis_index("core")
    entry_count, width = inputs.shape
    head_dim = HEAD_DIM
    query_width = query_weight.shape[1]
    pair_width = key_weight.shape[1]
    pair_heads = pair_width // head_dim
    query_heads = query_width // head_dim
    group_size = query_heads // pair_heads
    score_scale = head_dim ** (-0.5)
    hidden_units = gate_weight.shape[1]
    rows = gate_weight.shape[0]
    hidden_rows = down_weight.shape[0]
    hidden_chunk = hidden_units // n_ctx
    attention_width = query_width + 2 * pair_width

    def ctx_rows_gather(values):
        slots = [values] + [rotate(values, n_ctx, r) for r in range(1, n_ctx)]
        return in_order(slots, n_ctx, me).reshape(n_ctx * rows, -1)

    def plane_gather(values):
        return lax.all_gather(values, planes, axis=0, tiled=True)

    def plane_scatter(values):
        parts = values.reshape(n_chips, n_core, -1, values.shape[1])
        kept = lax.dynamic_index_in_dim(parts, core, 1, keepdims=False)
        if n_core == 2:
            sent = lax.dynamic_index_in_dim(parts, 1 - core, 1, keepdims=False).astype(LOW)
            came = lax.ppermute(sent, "core", [(0, 1), (1, 0)])
            kept = (kept.astype(WIDE) + came.astype(WIDE)).astype(LOW)
        return lax.psum_scatter(
            kept.reshape(-1, values.shape[1]), chips, scatter_dimension=0, tiled=True
        )

    gains = jnp.stack([attention_gain, feedforward_gain], 1)
    gains = jnp.pad(gains, ((0, 0), (0, LANES - 2)))
    first_low = jnp.concatenate([query_weight, key_weight, value_weight, gains], 1).astype(LOW)
    first_rows = ctx_rows_gather(first_low)
    first_full = plane_gather(first_rows)

    both = jnp.stack([gate_weight, up_weight], 1).astype(LOW)
    both = both.reshape(rows, 2, n_dp, n_ctx, hidden_rows)
    both = after(both, first_rows)

    def chunk_for(place):
        part = lax.dynamic_index_in_dim(both, place, 3, keepdims=False)
        return part.reshape(rows, 2 * hidden_chunk)

    both_slots = [chunk_for(me)] + [
        rotate(chunk_for(lax.rem(me + r, n_ctx)), n_ctx, r) for r in range(1, n_ctx)
    ]
    both_rows = in_order(both_slots, n_ctx, me).reshape(n_ctx * rows, 2 * hidden_chunk)

    output_rows = ctx_rows_gather(after(output_weight.astype(LOW), both_rows))
    output_full = plane_gather(output_rows)
    both_full = plane_gather(both_rows)
    down_full = plane_gather(after(down_weight.astype(LOW), both_rows))

    query_full = first_full[:, :query_width]
    key_full = first_full[:, query_width : query_width + pair_width]
    value_full = first_full[:, query_width + pair_width : attention_width]
    gain_first = first_full[:, attention_width].astype(WIDE)
    gain_second = first_full[:, attention_width + 1].astype(WIDE)

    spans = segment_ids[0]
    reality = real_entry_flags[0]
    opening = me * entry_count
    places = opening + jnp.arange(entry_count, dtype=jnp.int32)
    own_spans = lax.dynamic_slice_in_dim(spans, opening, entry_count)
    doc_starts = jnp.sum((spans[None, :] < own_spans[:, None]).astype(jnp.int32), axis=1)
    offsets = (places - doc_starts).astype(WIDE)
    half_dim = head_dim // 2
    frequency = ROPE_BASE ** (-(jnp.arange(half_dim, dtype=WIDE) * 2.0 / head_dim))
    angle = offsets[:, None, None] * frequency[None, None, :]
    cosine, sine = jnp.cos(angle), jnp.sin(angle)
    key_places, key_spans, key_reality = [], [], []
    for r in range(n_ctx):
        start = (me - r) * entry_count
        key_places.append(start + jnp.arange(entry_count, dtype=jnp.int32))
        start = jnp.maximum(start, 0)
        key_spans.append(lax.dynamic_slice_in_dim(spans, start, entry_count))
        key_reality.append(lax.dynamic_slice_in_dim(reality, start, entry_count))
    key_places = jnp.concatenate(key_places)
    key_spans = jnp.concatenate(key_spans)
    key_reality = jnp.concatenate(key_reality)
    allowed = (
        (own_spans[:, None] == key_spans[None, :])
        & (key_places[None, :] <= places[:, None])
        & (key_places[None, :] >= 0)
        & (key_reality[None, :] == 1)
    ) | (key_places[None, :] == places[:, None])

    tokens_wide = inputs.astype(WIDE)
    unit_first = tokens_wide * inverse_root(tokens_wide)
    first_hidden = (unit_first * gain_first).astype(LOW)
    keys_own = turn(
        matmul(first_hidden, key_full).reshape(entry_count, pair_heads, head_dim), cosine, sine
    )
    values_own = matmul(first_hidden, value_full)
    pair_own = jnp.concatenate(
        [keys_own.reshape(entry_count, pair_width).astype(LOW), values_own.astype(LOW)], 1
    )
    pair_slots = line_gather_up(pair_own, n_ctx)
    pair_all = jnp.concatenate(pair_slots, 0)
    seq_length = pair_all.shape[0]
    keys = pair_all[:, :pair_width].reshape(seq_length, pair_heads, head_dim)
    values = pair_all[:, pair_width:].reshape(seq_length, pair_heads, head_dim)
    queries = (
        turn(
            matmul(first_hidden, query_full).reshape(entry_count, query_heads, head_dim),
            cosine,
            sine,
        )
        .astype(LOW)
        .reshape(entry_count, pair_heads, group_size, head_dim)
    )

    def scores_of():
        raw = jnp.einsum("ikgd,jkd->kgij", queries, keys, preferred_element_type=WIDE)
        return jnp.where(allowed[None, None], raw * score_scale, MASKED_SCORE)

    scores = scores_of()
    row_top = jnp.max(scores, axis=-1, keepdims=True)
    exponent = jnp.exp(scores - row_top)
    row_total = jnp.sum(exponent, axis=-1, keepdims=True)
    log_total = row_top + jnp.log(row_total)
    probs_low = (exponent / row_total).astype(LOW)
    attended = (
        jnp.einsum("kgij,jkd->ikgd", probs_low, values, preferred_element_type=WIDE)
        .reshape(entry_count, query_width)
        .astype(LOW)
    )

    residual = tokens_wide + matmul(attended, output_full)
    unit_second = residual * inverse_root(residual)
    second_hidden = (unit_second * gain_second).astype(LOW)
    cot_slots = line_gather(after(cotangent, output_rows, pair_all), n_ctx, me)
    cot_all = jnp.concatenate(cot_slots, 0)
    hidden_all = jnp.concatenate(line_gather(second_hidden, n_ctx, me), 0)
    grad_active = matmul_right_t(cot_all, down_full)
    gate_value = matmul(hidden_all, both_full[:, :hidden_chunk])
    up_value = matmul(hidden_all, both_full[:, hidden_chunk:])
    sigmoid_gate = jax.nn.sigmoid(gate_value)
    active = (gate_value * sigmoid_gate * up_value).astype(LOW)
    grad_gate = (
        grad_active * up_value * sigmoid_gate * (1.0 + gate_value * (1.0 - sigmoid_gate))
    ).astype(LOW)
    grad_up = (grad_active * gate_value * sigmoid_gate).astype(LOW)
    grad_both = jnp.concatenate([grad_gate, grad_up], 1)

    second_parts = matmul_right_t(grad_both, both_full)
    grad_second = line_scatter(
        [second_parts[r * entry_count : (r + 1) * entry_count] for r in range(n_ctx)], n_ctx
    )
    down_parts = matmul(after(active, grad_second), down_full)
    down_value = line_scatter(
        [down_parts[r * entry_count : (r + 1) * entry_count] for r in range(n_ctx)], n_ctx
    )
    block_output = (residual + down_value).astype(LOW)

    down_weight_grad = plane_scatter(matmul_left_t(active, cot_all).astype(LOW)).astype(WIDE)
    both_grad_rows = plane_scatter(matmul_left_t(hidden_all, grad_both).astype(LOW))
    both_grad_parts = both_grad_rows.reshape(n_ctx, rows, 2 * hidden_chunk)
    part_for = lambda place: lax.dynamic_index_in_dim(both_grad_parts, place, 0, keepdims=False)
    grad_slots = [part_for(me)] + [
        rotate(part_for(lax.rem(me + r, n_ctx)), n_ctx, r) for r in range(1, n_ctx)
    ]
    both_grad = in_order(grad_slots, n_ctx, me).reshape(n_ctx, rows, 2, n_dp, hidden_rows)
    both_grad = both_grad.transpose(2, 1, 3, 0, 4).reshape(2, rows, hidden_units).astype(WIDE)
    gate_weight_grad, up_weight_grad = both_grad[0], both_grad[1]

    second_gain_term = jnp.sum(grad_second * unit_second, axis=0)
    grad_residual = cotangent.astype(WIDE) + norm_back(residual, grad_second * gain_second)
    grad_branch = grad_residual.astype(LOW)
    grad_attended = (
        matmul_right_t(grad_branch, output_full)
        .astype(LOW)
        .reshape(entry_count, pair_heads, group_size, head_dim)
    )
    probs = jnp.exp(scores_of() - log_total)
    grad_probs = jnp.einsum("ikgd,jkd->kgij", grad_attended, values, preferred_element_type=WIDE)
    row_delta = jnp.sum(probs * grad_probs, axis=-1, keepdims=True)
    grad_scores = (probs * (grad_probs - row_delta)).astype(LOW)
    key_part = (
        jnp.einsum("kgij,ikgd->jkd", grad_scores, queries, preferred_element_type=WIDE)
        * score_scale
    ).reshape(seq_length, pair_width)
    value_part = jnp.einsum(
        "kgij,ikgd->jkd", probs_low, grad_attended, preferred_element_type=WIDE
    ).reshape(seq_length, pair_width)
    pair_part = jnp.concatenate([key_part, value_part], 1)
    pair_grad = line_scatter_down(
        [pair_part[r * entry_count : (r + 1) * entry_count] for r in range(n_ctx)], n_ctx
    )
    grad_queries_rot = (
        jnp.einsum("kgij,jkd->ikgd", grad_scores, keys, preferred_element_type=WIDE) * score_scale
    )
    grad_query = (
        turn(grad_queries_rot.reshape(entry_count, query_heads, head_dim), cosine, -sine)
        .astype(LOW)
        .reshape(entry_count, query_width)
    )
    grad_key = (
        turn(
            pair_grad[:, :pair_width].reshape(entry_count, pair_heads, head_dim), cosine, -sine
        )
        .astype(LOW)
        .reshape(entry_count, pair_width)
    )
    grad_value = pair_grad[:, pair_width:].astype(LOW)
    grad_qkv = jnp.concatenate([grad_query, grad_key, grad_value], 1)
    grad_first = matmul_right_t(grad_qkv, first_full[:, :attention_width])
    first_gain_term = jnp.sum(grad_first * unit_first, axis=0)
    input_grad = (grad_residual + norm_back(tokens_wide, grad_first * gain_first)).astype(LOW)

    def ctx_rows_scatter(values):
        parts = values.reshape(n_ctx, rows, values.shape[1])
        get = lambda place: lax.dynamic_index_in_dim(parts, place, 0, keepdims=False)
        total = get(me).astype(WIDE)
        for r in range(1, n_ctx):
            total = total + rotate(get(lax.rem(me + r, n_ctx)), n_ctx, r).astype(WIDE)
        return total

    output_weight_grad = ctx_rows_scatter(
        plane_scatter(matmul_left_t(attended, grad_branch).astype(LOW))
    )
    gain_terms = jnp.pad(
        jnp.stack([first_gain_term, second_gain_term], 1), ((0, 0), (0, LANES - 2))
    )
    first_grad = ctx_rows_scatter(
        plane_scatter(
            jnp.concatenate([matmul_left_t(first_hidden, grad_qkv), gain_terms], 1).astype(LOW)
        )
    )
    return (
        block_output,
        input_grad,
        first_grad[:, attention_width],
        first_grad[:, attention_width + 1],
        first_grad[:, :query_width],
        first_grad[:, query_width : query_width + pair_width],
        first_grad[:, query_width + pair_width : attention_width],
        output_weight_grad,
        gate_weight_grad,
        up_weight_grad,
        down_weight_grad,
    )


def solution(mesh):
    n_dp, n_ctx = mesh.shape["dp"], mesh.shape["ctx"]
    n_core = 2 if n_dp % 2 == 0 else 1
    n_chips = n_dp // n_core
    n_y = math.isqrt(n_chips)
    while n_chips % n_y:
        n_y -= 1
    axes = ("y", "x", "core", "ctx")
    fine = Mesh(mesh.devices.reshape(n_y, n_chips // n_y, n_core, n_ctx), axes)
    matrix = P(axes, None)
    vector = P(axes)
    per_sequence = P(("y", "x", "core"), None)
    return jax.shard_map(
        per_device,
        mesh=fine,
        in_specs=(matrix, matrix, per_sequence, per_sequence, vector, vector) + (matrix,) * 7,
        out_specs=(matrix, matrix, vector, vector) + (matrix,) * 7,
        check_vma=False,
    )
```

```python
import math

import jax
import jax.numpy as jnp
from jax import lax
from jax.experimental import pallas as pl
from jax.experimental.pallas import tpu as pltpu
from jax.sharding import Mesh
from jax.sharding import PartitionSpec as P

HEAD_DIM = 64
EPSILON = 1e-05
ROPE_BASE = 500000.0
MASKED_SCORE = -1e30
LANES = 128
GROUP = 4
SCORE_SCALE = HEAD_DIM**-0.5
KERNEL_MEMORY = 40 * 2**20
FEED_MEMORY = 56 * 2**20
FEED_STEP = 256
BACK_COST = pl.CostEstimate(flops=24_000_000_000, bytes_accessed=10_000_000, transcendentals=0)
COST = pl.CostEstimate(flops=1_000_000, bytes_accessed=1_000_000, transcendentals=0)

LOW = jnp.bfloat16
WIDE = jnp.float32
NN = (((1,), (0,)), ((), ()))
NT = (((1,), (1,)), ((), ()))
TN = (((0,), (0,)), ((), ()))


def dot(left, right, dims):
    return lax.dot_general(left, right, dims, preferred_element_type=WIDE)


def inverse_root(values):
    return lax.rsqrt(jnp.mean(values * values, axis=-1, keepdims=True) + EPSILON)


def norm_back(values, grad_normed):
    scaled = inverse_root(values)
    unit_rows = values * scaled
    return scaled * (
        grad_normed - unit_rows * jnp.mean(grad_normed * unit_rows, axis=-1, keepdims=True)
    )


def tie_kernel(*refs):
    del refs


def after(values, *earlier):
    anywhere = pl.BlockSpec(memory_space=pl.ANY)
    return pl.pallas_call(
        tie_kernel,
        in_specs=[anywhere] * (1 + len(earlier)),
        out_specs=anywhere,
        out_shape=jax.ShapeDtypeStruct(values.shape, values.dtype),
        input_output_aliases={0: 0},
        name="after",
    )(values, *earlier)


def turned(values, cosine, sine, first_half):
    ahead = pltpu.roll(values, LANES - HEAD_DIM // 2, 1)
    behind = pltpu.roll(values, HEAD_DIM // 2, 1)
    return values * cosine + jnp.where(first_half, ahead, behind) * sine


def lane_index():
    return lax.broadcasted_iota(jnp.int32, (1, LANES), 1)


def first_half_lanes():
    return lax.rem(lane_index(), HEAD_DIM) < HEAD_DIM // 2


def placed(block, member, head):
    start = member * GROUP * HEAD_DIM + (head // 2) * LANES
    values = block[:, start : start + LANES]
    if head % 2 != member:
        values = pltpu.roll(values, HEAD_DIM, 1)
    own = (lane_index() >= HEAD_DIM) if member else (lane_index() < HEAD_DIM)
    return jnp.where(own, values, jnp.zeros_like(values))


def forward_kernel(
    raw_ref, cos_ref, sin_ref, key_ref, value_ref, bias_ref, query_ref, out_ref, log_ref
):
    half = first_half_lanes()
    cosine, sine = cos_ref[...], sin_ref[...]
    wide = raw_ref.shape[1]
    block = jnp.concatenate(
        [
            turned(raw_ref[:, c : c + LANES], cosine, sine, half).astype(LOW).astype(WIDE)
            * SCORE_SCALE
            for c in range(0, wide, LANES)
        ],
        1,
    )
    query_ref[...] = block.astype(LOW)
    keys, values = key_ref[...], value_ref[...]
    span = GROUP * HEAD_DIM
    for member in range(2):
        parts = []
        for head in range(GROUP):
            query = placed(block, member, head).astype(LOW)
            scores = dot(keys, query, NT) + bias_ref[...]
            top = jnp.max(scores, 0, keepdims=True)
            exponent = jnp.exp(scores - top)
            total = jnp.sum(exponent, 0, keepdims=True)
            mixed = dot(values, exponent.astype(LOW), TN)
            parts.append(mixed[member * HEAD_DIM : (member + 1) * HEAD_DIM] / total)
            row = member * GROUP + head
            log_ref[row : row + 1, :] = top + jnp.log(total)
        out_ref[:, member * span : (member + 1) * span] = jnp.concatenate(parts, 0).T.astype(LOW)


def backward_kernel(
    query_ref,
    cos_ref,
    sin_ref,
    key_ref,
    value_ref,
    bias_ref,
    grad_ref,
    out_ref,
    log_ref,
    grad_query_ref,
    grad_key_ref,
    grad_value_ref,
):
    half = first_half_lanes()
    cosine, sine = cos_ref[...], -sin_ref[...]
    block = query_ref[...].astype(WIDE)
    grad = grad_ref[...].astype(WIDE)
    product = grad * out_ref[...].astype(WIDE)
    keys, values = key_ref[...], value_ref[...]
    span = GROUP * HEAD_DIM
    grad_keys = grad_values = None
    for member in range(2):
        parts = []
        product_t = product[:, member * span : (member + 1) * span].T
        for head in range(GROUP):
            query = placed(block, member, head).astype(LOW)
            grad_out = placed(grad, member, head).astype(LOW)
            row = member * GROUP + head
            delta = jnp.sum(
                product_t[head * HEAD_DIM : (head + 1) * HEAD_DIM], 0, keepdims=True
            )
            scores = dot(keys, query, NT) + bias_ref[...]
            probs = jnp.exp(scores - log_ref[row : row + 1, :])
            grad_probs = dot(values, grad_out, NT)
            grad_scores = (probs * (grad_probs - delta)).astype(LOW)
            key_part = dot(grad_scores, query, NN)
            value_part = dot(probs.astype(LOW), grad_out, NN)
            grad_keys = key_part if grad_keys is None else grad_keys + key_part
            grad_values = value_part if grad_values is None else grad_values + value_part
            query_part = dot(keys, grad_scores, TN)
            parts.append(query_part[member * HEAD_DIM : (member + 1) * HEAD_DIM] * SCORE_SCALE)
        grad_query = jnp.concatenate(parts, 0).T
        for c in range(0, span, LANES):
            grad_query_ref[:, member * span + c : member * span + c + LANES] = turned(
                grad_query[:, c : c + LANES], cosine, sine, half
            ).astype(LOW)
    grad_key_ref[...] = grad_keys.astype(LOW)
    grad_value_ref[...] = grad_values.astype(LOW)


def turn_kernel(values_ref, cos_ref, sin_ref, out_ref):
    half = first_half_lanes()
    width = values_ref.shape[1]
    for c in range(0, width // 2, LANES):
        out_ref[:, c : c + LANES] = turned(
            values_ref[:, c : c + LANES], cos_ref[...], sin_ref[...], half
        ).astype(LOW)
    out_ref[:, width // 2 :] = values_ref[:, width // 2 :].astype(LOW)


def feed_kernel(
    token_ref, goal_ref, gate_ref, up_ref, down_ref, active_ref, grad_gate_ref, grad_up_ref
):
    gate, up = dot(token_ref[...], gate_ref[...], NN), dot(token_ref[...], up_ref[...], NN)
    grad_active = dot(goal_ref[...], down_ref[...], NT)
    sigmoid = 1.0 / (1.0 + jnp.exp(-gate))
    silu = gate * sigmoid
    active_ref[...] = (silu * up).astype(LOW)
    grad_gate_ref[...] = (grad_active * up * sigmoid * (1.0 + gate * (1.0 - sigmoid))).astype(LOW)
    grad_up_ref[...] = (grad_active * silu).astype(LOW)


def second_kernel(grad_gate_ref, grad_up_ref, gate_ref, up_ref, out_ref):
    out_ref[...] = (
        dot(grad_gate_ref[...], gate_ref[...], NT) + dot(grad_up_ref[...], up_ref[...], NT)
    ).astype(LOW)


def feed_specs(count, width):
    whole = pl.BlockSpec((count, width), lambda i: (0, 0))
    return whole, pl.BlockSpec((count, FEED_STEP), lambda i: (0, i))


def feed(tokens, goal, both, down):
    count, width = tokens.shape
    hidden = down.shape[0]
    steps = hidden // FEED_STEP
    whole, part = feed_specs(count, width)
    return pl.pallas_call(
        feed_kernel,
        grid=(steps,),
        in_specs=[
            whole,
            whole,
            pl.BlockSpec((width, FEED_STEP), lambda i: (0, i)),
            pl.BlockSpec((width, FEED_STEP), lambda i: (0, i + steps)),
            pl.BlockSpec((FEED_STEP, width), lambda i: (i, 0)),
        ],
        out_specs=[part, part, part],
        out_shape=[jax.ShapeDtypeStruct((count, hidden), LOW)] * 3,
        compiler_params=pltpu.CompilerParams(vmem_limit_bytes=FEED_MEMORY),
        cost_estimate=COST,
        name="feed",
    )(tokens, goal, both, both, down)


def feed_back(grad_gate, grad_up, both):
    count, hidden = grad_gate.shape
    width = both.shape[0]
    whole, part = feed_specs(count, hidden)
    return pl.pallas_call(
        second_kernel,
        grid=(width // FEED_STEP,),
        in_specs=[
            whole,
            whole,
            pl.BlockSpec((FEED_STEP, hidden), lambda i: (i, 0)),
            pl.BlockSpec((FEED_STEP, hidden), lambda i: (i, 1)),
        ],
        out_specs=part,
        out_shape=jax.ShapeDtypeStruct((count, width), LOW),
        compiler_params=pltpu.CompilerParams(vmem_limit_bytes=FEED_MEMORY),
        cost_estimate=COST,
        name="feed_back",
    )(grad_gate, grad_up, both, both)


def weight_kernel(shared, parts, core_ref, *refs):
    del core_ref
    sides = max(shared) + 1
    lefts, rest = refs[: sides * parts], refs[sides * parts :]
    rights, out_ref = rest[: len(shared) * parts], rest[-1]
    came_ref = rest[-2] if len(rest) > len(shared) * parts + 1 else None
    for kind, side in enumerate(shared):

        @pl.when(pl.program_id(1) == kind)
        def _():
            total = None
            for part in range(parts):
                term = dot(
                    lefts[side * parts + part][...], rights[kind * parts + part][...], TN
                )
                total = term if total is None else total + term
            if came_ref is not None:
                total = total + came_ref[...].astype(WIDE)
            out_ref[...] = total.astype(LOW)


def weight_rows(lefts, rights, shared, index, chips, n_core, came=None):
    tokens, columns = rights[0][0].shape
    kinds, parts = len(rights), len(rights[0])
    size = lefts[0][0].shape[1] // (chips * n_core)
    left = pl.BlockSpec((tokens, size), lambda i, g, core: (0, i * n_core + core[0]))
    right = pl.BlockSpec((tokens, columns), lambda i, g, core: (0, 0))
    out = pl.BlockSpec((size, columns), lambda i, g, core: (i * kinds + g, 0))
    return pl.pallas_call(
        lambda *refs: weight_kernel(shared, parts, *refs),
        grid_spec=pltpu.PrefetchScalarGridSpec(
            num_scalar_prefetch=1,
            grid=(chips, kinds),
            in_specs=[left] * (parts * len(lefts))
            + [right] * (kinds * parts)
            + ([] if came is None else [out]),
            out_specs=out,
        ),
        out_shape=jax.ShapeDtypeStruct((chips * kinds * size, columns), LOW),
        compiler_params=pltpu.CompilerParams(vmem_limit_bytes=FEED_MEMORY),
        cost_estimate=pl.CostEstimate(
            flops=2 * chips * kinds * size * columns * tokens * parts,
            bytes_accessed=2 * chips * kinds * size * columns,
            transcendentals=0,
        ),
        name="weight_rows",
    )(
        jnp.reshape(index, (1,)).astype(jnp.int32),
        *(part for side in lefts for part in side),
        *(part for kind in rights for part in kind),
        *([] if came is None else [came]),
    )


def fixed_block(shape):
    return pl.BlockSpec(shape, lambda i: (0, 0))


def attention_blocks(count, length, steps):
    span = 2 * GROUP * HEAD_DIM
    return (
        pl.BlockSpec((count, span), lambda i: (0, i)),
        pl.BlockSpec((length, LANES), lambda i: (0, i)),
        pl.BlockSpec((length, LANES), lambda i: (0, i + steps)),
        pl.BlockSpec((2 * GROUP, count), lambda i: (i, 0)),
    )


def attend(raw, cosine, sine, pair, bias):
    count, length = raw.shape[0], pair.shape[0]
    steps = pair.shape[1] // 2 // LANES
    wide, key, value, rows = attention_blocks(count, length, steps)
    table = fixed_block((count, LANES))
    return pl.pallas_call(
        forward_kernel,
        grid=(steps,),
        in_specs=[wide, table, table, key, value, fixed_block((length, count))],
        out_specs=[wide, wide, rows],
        out_shape=[
            jax.ShapeDtypeStruct(raw.shape, LOW),
            jax.ShapeDtypeStruct(raw.shape, LOW),
            jax.ShapeDtypeStruct((steps * 2 * GROUP, count), WIDE),
        ],
        compiler_params=pltpu.CompilerParams(vmem_limit_bytes=KERNEL_MEMORY),
        cost_estimate=COST,
        name="attend",
    )(raw, cosine, sine, pair, pair, bias)


def attend_back(query, cosine, sine, pair, bias, grad, out, log_total):
    count, length = query.shape[0], pair.shape[0]
    steps = pair.shape[1] // 2 // LANES
    wide, key, value, rows = attention_blocks(count, length, steps)
    table = fixed_block((count, LANES))
    half = jax.ShapeDtypeStruct((length, steps * LANES), LOW)
    return pl.pallas_call(
        backward_kernel,
        grid=(steps,),
        in_specs=[wide, table, table, key, value, fixed_block((length, count)), wide, wide, rows],
        out_specs=[wide, key, key],
        out_shape=[jax.ShapeDtypeStruct(query.shape, LOW), half, half],
        compiler_params=pltpu.CompilerParams(vmem_limit_bytes=KERNEL_MEMORY),
        cost_estimate=BACK_COST,
        name="attend_back",
    )(query, cosine, sine, pair, pair, bias, grad, out, log_total)


def turn_pair(values, cosine, sine):
    return pl.pallas_call(
        turn_kernel, out_shape=jax.ShapeDtypeStruct(values.shape, LOW), name="turn_pair"
    )(values, cosine, sine)


def shift(values, count, step, senders):
    pairs = [(i, i + step) for i in senders if 0 <= i + step < count]
    return lax.ppermute(values, "ctx", pairs)


def rotate(values, count, step):
    return lax.ppermute(values, "ctx", [(i, (i + step) % count) for i in range(count)])


def line_slot(up, down, count, me, r):
    return up[0] if r == 0 else jnp.where(me >= r, up[r], down[count - r])


def line_chains(own, count):
    up, down = [own], [own]
    for s in range(1, count):
        up.append(shift(up[-1], count, 1, range(s - 1, count)))
        down.append(shift(down[-1], count, -1, range(0, count - s + 1)))
    return up, down


def line_groups(count):
    first = [r for r in range(count) if r == 0 or max(r, count - r) < count - 1]
    groups = [first, [r for r in range(count) if r not in first]]
    return [group for group in groups if group]


def line_step(slots, count, step, came):
    up, down = slots[step], slots[count - step]
    if came is not None:
        up = (up.astype(WIDE) + came[0].astype(WIDE)).astype(LOW)
        down = (down.astype(WIDE) + came[1].astype(WIDE)).astype(LOW)
    return up, down


def line_send(pair, count, step):
    up = shift(pair[0], count, 1, range(0, step))
    return up, shift(pair[1], count, -1, range(count - step, count))


def line_gather_up(own, count):
    return [own] + [shift(own, count, s, range(count)) for s in range(1, count)]


def in_order(slots, count, me):
    out = jnp.zeros((count, *slots[0].shape), slots[0].dtype)
    for r in range(count):
        out = lax.dynamic_update_index_in_dim(out, slots[r], lax.rem(me - r + count, count), 0)
    return out


CHIPS = ("y", "x")
PLANES = ("y", "x", "core")
SWAP = [(0, 1), (1, 0)]


def pick(values, index, axis):
    return lax.dynamic_index_in_dim(values, index, axis, keepdims=False)


def small_square():
    return lax.axis_size("y") == 2 and lax.axis_size("x") == 2 and lax.axis_size("core") == 2


def plane_gather(values):
    return lax.all_gather(values, PLANES, axis=0, tiled=True)


def core_columns(values, index):
    n_core, chips = lax.axis_size("core"), lax.axis_size(CHIPS)
    size = values.shape[1] // (chips * n_core)
    return jnp.concatenate(
        [
            lax.dynamic_slice_in_dim(values, (chip * n_core + index) * size, size, 1)
            for chip in range(chips)
        ],
        1,
    )


def core_term(left, right):
    if lax.axis_size("core") == 1:
        return None
    return dot(core_columns(left, 1 - lax.axis_index("core")), right, TN).astype(LOW)


def core_summed(left, right, sent=None):
    if lax.axis_size("core") == 1:
        return dot(left, right, TN).astype(LOW)
    sent = core_term(left, right) if sent is None else sent
    came = lax.ppermute(sent, "core", SWAP)
    own = core_columns(left, lax.axis_index("core"))
    return (dot(own, right, TN) + came.astype(WIDE)).astype(LOW)


def group_terms(lefts, rights, shared):
    n_core, chips = lax.axis_size("core"), lax.axis_size(CHIPS)
    core = lax.axis_index("core")
    size = lefts[0][0].shape[1] // (chips * n_core)
    if n_core == 2 and size % LANES == 0:
        sent = weight_rows(lefts, rights, shared, 1 - core, chips, n_core)

        def summed(tied, last=()):
            came = lax.ppermute(after(sent, *tied), "core", SWAP)
            came = after(came, *last) if last else came
            return weight_rows(lefts, rights, shared, core, chips, n_core, came)

        return sent, summed
    each = [
        core_summed(jnp.concatenate(lefts[side], 0), jnp.concatenate(kind, 0))
        for kind, side in zip(rights, shared)
    ]
    each = jnp.concatenate([values.reshape(chips, 1, size, -1) for values in each], 1)
    each = each.reshape(chips * len(rights) * size, -1)
    return each, lambda tied, last=(): each


def chip_scatter(values):
    return lax.psum_scatter(values, CHIPS, scatter_dimension=0, tiled=True)


def chip_scatter_steps(values, *between):
    if not small_square():
        return chip_scatter(values)
    columns = values.shape[1]
    y, x = lax.axis_index("y"), lax.axis_index("x")
    parts = values.reshape(2, 2, -1, columns)
    half = parts.shape[2] // 2
    add = lambda a, b: (a.astype(WIDE) + b.astype(WIDE)).astype(LOW)
    top, bottom = parts[:, :, :half], parts[:, :, half:]
    top_came = lax.ppermute(pick(top, 1 - x, 1), "x", SWAP)
    bottom_came = lax.ppermute(pick(bottom, 1 - y, 0), "y", SWAP)
    top = after(add(pick(top, x, 1), top_came), *between)
    bottom = add(pick(bottom, y, 0), bottom_came)
    top_came = lax.ppermute(pick(top, 1 - y, 0), "y", SWAP)
    bottom_came = lax.ppermute(pick(bottom, 1 - x, 0), "x", SWAP)
    top = add(pick(top, y, 0), top_came)
    bottom = add(pick(bottom, x, 0), bottom_came)
    return jnp.concatenate([top, bottom], 0)


def per_device(
    inputs,
    cotangent,
    segment_ids,
    real_entry_flags,
    attention_gain,
    feedforward_gain,
    query_weight,
    key_weight,
    value_weight,
    output_weight,
    gate_weight,
    up_weight,
    down_weight,
):
    n_ctx = lax.axis_size("ctx")
    n_dp = lax.axis_size(PLANES)
    me = lax.axis_index("ctx")
    entry_count, width = inputs.shape
    query_width = query_weight.shape[1]
    pair_width = key_weight.shape[1]
    hidden_units = gate_weight.shape[1]
    rows = gate_weight.shape[0]
    hidden_rows = down_weight.shape[0]
    hidden_chunk = hidden_units // n_ctx

    def ctx_rows_gather(values):
        slots = [values] + [rotate(values, n_ctx, r) for r in range(1, n_ctx)]
        return in_order(slots, n_ctx, me).reshape(n_ctx * rows, -1)

    gains = jnp.pad(
        jnp.stack([attention_gain, feedforward_gain], 1), ((0, 0), (0, LANES - 2))
    )
    pair_low = jnp.concatenate([key_weight, value_weight, gains], 1).astype(LOW)
    pair_rows = ctx_rows_gather(pair_low)
    pair_full = plane_gather(pair_rows)

    branch_low = jnp.concatenate([query_weight, output_weight], 1).astype(LOW)
    branch_rows = ctx_rows_gather(after(branch_low, pair_rows))
    branch_full = plane_gather(branch_rows)

    both = jnp.stack([gate_weight, up_weight], 1).astype(LOW)
    both = both.reshape(rows, 2, n_dp, n_ctx, hidden_rows)
    chunk_for = lambda place: pick(both, place, 3).reshape(rows, 2 * hidden_chunk)

    gain_first = pair_full[:, 2 * pair_width].astype(WIDE)
    gain_second = pair_full[:, 2 * pair_width + 1].astype(WIDE)
    pair_weight = pair_full[:, : 2 * pair_width]
    query_full = branch_full[:, :query_width]
    output_full = branch_full[:, query_width:]

    spans = segment_ids[0]
    reality = real_entry_flags[0]
    opening = me * entry_count
    places = opening + jnp.arange(entry_count, dtype=jnp.int32)
    own_spans = lax.dynamic_slice_in_dim(spans, opening, entry_count)
    doc_starts = jnp.sum((spans[None, :] < own_spans[:, None]).astype(jnp.int32), axis=1)
    offsets = (places - doc_starts).astype(WIDE)
    frequency = ROPE_BASE ** (
        -(jnp.arange(HEAD_DIM // 2, dtype=WIDE) * 2.0 / HEAD_DIM)
    )
    angle = offsets[:, None] * frequency[None, :]
    cosine, sine = jnp.cos(angle), jnp.sin(angle)
    cosine = jnp.concatenate([cosine] * 4, 1)
    sine = jnp.concatenate([-sine, sine] * 2, 1)
    key_places, key_spans, key_reality = [], [], []
    for r in range(n_ctx):
        start = (me - r) * entry_count
        key_places.append(start + jnp.arange(entry_count, dtype=jnp.int32))
        start = jnp.maximum(start, 0)
        key_spans.append(lax.dynamic_slice_in_dim(spans, start, entry_count))
        key_reality.append(lax.dynamic_slice_in_dim(reality, start, entry_count))
    key_places = jnp.concatenate(key_places)[:, None]
    key_spans = jnp.concatenate(key_spans)[:, None]
    key_reality = jnp.concatenate(key_reality)[:, None]
    allowed = (
        (own_spans[None, :] == key_spans)
        & (key_places <= places[None, :])
        & (key_places >= 0)
        & (key_reality == 1)
    ) | (key_places == places[None, :])
    bias = jnp.where(allowed, 0.0, MASKED_SCORE).astype(WIDE)

    tokens_wide = inputs.astype(WIDE)
    unit_first = tokens_wide * inverse_root(tokens_wide)
    first_hidden = (unit_first * gain_first).astype(LOW)
    both_slots = [chunk_for(me)] + [
        rotate(after(chunk_for(lax.rem(me + r, n_ctx)), branch_rows), n_ctx, r)
        for r in range(1, n_ctx)
    ]
    both_rows = in_order(both_slots, n_ctx, me).reshape(n_ctx * rows, 2 * hidden_chunk)
    both_full = plane_gather(both_rows)
    down_full = plane_gather(after(down_weight.astype(LOW), branch_rows))
    pair_own = turn_pair(dot(first_hidden, pair_weight, NN), cosine, sine)
    pair_all = jnp.concatenate(line_gather_up(after(pair_own, both_rows), n_ctx), 0)
    cot_sent = after(cotangent, pair_all)
    cot_slots = [cotangent] + [rotate(cot_sent, n_ctx, r) for r in range(1, n_ctx)]
    raw_query = dot(first_hidden, query_full, NN)
    query, attended, log_total = attend(raw_query, cosine, sine, pair_all, bias)

    residual = tokens_wide + dot(attended, output_full, NN)
    unit_second = residual * inverse_root(residual)
    second_hidden = (unit_second * gain_second).astype(LOW)
    up_chain, down_chain = line_chains(after(second_hidden, *cot_slots[1:]), n_ctx)
    groups = line_groups(n_ctx)
    hidden, cot, active, gates, ups = [], [], [], [], []
    second_slots, down_slots = [None] * n_ctx, [None] * n_ctx
    for group in groups:
        tokens = jnp.concatenate(
            [line_slot(up_chain, down_chain, n_ctx, me, r) for r in group], 0
        )
        goal = jnp.concatenate([cot_slots[r] for r in group], 0)
        if active:
            goal = after(goal, active[-1])
        group_active, grad_gate, grad_up = feed(tokens, goal, both_full, down_full)
        second = feed_back(grad_gate, grad_up, both_full)
        for k, r in enumerate(group):
            second_slots[r] = second[k * entry_count : (k + 1) * entry_count]
        for kept, value in zip(
            (hidden, cot, active, gates, ups), (tokens, goal, group_active, grad_gate, grad_up)
        ):
            kept.append(value)

    def down_terms(k, *tied):
        down_out = dot(after(active[k], *tied), down_full, NN).astype(LOW)
        for i, r in enumerate(groups[k]):
            down_slots[r] = down_out[i * entry_count : (i + 1) * entry_count]
        return down_out

    first = line_step(second_slots, n_ctx, 1, None)
    came, steps = line_send(first, n_ctx, 1), [first]
    early = down_terms(-1, *first)
    for step in range(2, n_ctx):
        sent = line_step(second_slots, n_ctx, step, came)
        if step == 2:
            sent = after(sent[0], early), sent[1]
        steps.append(sent)
        came = line_send(sent, n_ctx, step)
    gates[0] = after(gates[0], *steps[min(1, n_ctx - 2)])
    feed_sent, feed_summed = group_terms([hidden, active], [gates, ups, cot], [0, 0, 1])
    if len(groups) > 1:
        late = down_terms(0, *steps[-1])
        came = after(came[0], late), came[1]
    grad_second = second_slots[0].astype(WIDE) + came[0].astype(WIDE) + came[1].astype(WIDE)
    down_sent = tuple(
        after(values, grad_second) for values in line_step(down_slots, n_ctx, 1, None)
    )
    feed_part = feed_summed(steps[-1], down_sent)
    in_slots = lambda values: [
        values[r * entry_count : (r + 1) * entry_count] for r in range(n_ctx)
    ]
    feed_rows = chip_scatter(feed_part).reshape(3, n_ctx * rows, hidden_chunk)
    both_grad_rows = feed_rows[:2]
    down_weight_grad = feed_rows[2].astype(WIDE)

    both_grad_parts = both_grad_rows.reshape(2, n_ctx, rows, hidden_chunk)
    part_for = lambda place: pick(both_grad_parts, place, 1).reshape(2 * rows, hidden_chunk)
    grad_slots = [part_for(me)] + [
        rotate(part_for(lax.rem(me + r, n_ctx)), n_ctx, r) for r in range(1, n_ctx)
    ]

    second_gain_term = jnp.sum(grad_second * unit_second, axis=0)
    grad_residual = cotangent.astype(WIDE) + norm_back(residual, grad_second * gain_second)
    grad_branch = grad_residual.astype(LOW)
    grad_attended = after(dot(grad_branch, output_full, NT).astype(LOW), feed_part)
    down_came = None
    for step in range(1, n_ctx - 1):
        if step > 1:
            down_sent = line_step(down_slots, n_ctx, step, down_came)
            grad_attended = after(grad_attended, *down_sent)
        down_came = line_send(down_sent, n_ctx, step)
    grad_query, key_part, value_part = attend_back(
        query, cosine, sine, pair_all, bias, grad_attended, attended, log_total
    )
    pair_part = jnp.concatenate([key_part, value_part], 1)
    pair_part = jnp.concatenate([key_part, value_part], 1)
    if down_came is not None:
        down_came = tuple(after(values, grad_query) for values in down_came)
        down_sent = line_step(down_slots, n_ctx, n_ctx - 1, down_came)
    pair_part = after(pair_part, *down_sent)
    pair_slots = in_slots(pair_part)
    came, steps = None, []
    for step in range(1, n_ctx):
        sent = pair_slots[n_ctx - step]
        if came is not None:
            sent = (sent.astype(WIDE) + came.astype(WIDE)).astype(LOW)
        steps.append(sent)
        came = shift(sent, n_ctx, -1, range(n_ctx - step, n_ctx))
    pair_grad = pair_slots[0].astype(WIDE) + came.astype(WIDE)
    _, branch_summed = group_terms(
        [[attended], [first_hidden]],
        [[after(grad_branch, steps[min(1, n_ctx - 2)])], [grad_query]],
        [0, 1],
    )
    branch_terms = branch_summed([steps[-1]])
    grad_pair = turn_pair(after(pair_grad, grad_slots[n_ctx // 2]), cosine, -sine)
    grad_first = dot(grad_query, query_full, NT) + dot(grad_pair, pair_weight, NT)
    first_gain_term = jnp.sum(grad_first * unit_first, axis=0)
    input_grad = (grad_residual + norm_back(tokens_wide, grad_first * gain_first)).astype(LOW)

    def ctx_rows_scatter(values, *earlier):
        parts = values.reshape(n_ctx, -1, values.shape[1])
        total = pick(parts, me, 0).astype(WIDE)
        for r in range(1, n_ctx):
            came = rotate(pick(parts, lax.rem(me + r, n_ctx), 0), n_ctx, r)
            total = total + (after(came, *earlier) if earlier else came).astype(WIDE)
        return total

    branch_part = chip_scatter(branch_terms)
    gain_terms = jnp.pad(
        jnp.stack([first_gain_term, second_gain_term], 1), ((0, 0), (0, LANES - 2))
    ).astype(LOW)
    gain_parts = gain_terms.reshape(lax.axis_size(CHIPS), lax.axis_size("core"), -1, LANES)
    gain_part = pick(gain_parts, lax.axis_index("core"), 1)
    if lax.axis_size("core") == 2:
        gain_came = lax.ppermute(pick(gain_parts, 1 - lax.axis_index("core"), 1), "core", SWAP)
        gain_part = (gain_part.astype(WIDE) + gain_came.astype(WIDE)).astype(LOW)
    pair_terms = jnp.concatenate(
        [core_summed(first_hidden, grad_pair), gain_part.reshape(-1, LANES)], 1
    )
    pair_sum = chip_scatter_steps(pair_terms, *grad_slots[1:])
    pair_weight_grad = ctx_rows_scatter(pair_sum)
    grad_slots[0] = after(grad_slots[0], pair_weight_grad)
    both_grad = in_order(grad_slots, n_ctx, me).reshape(n_ctx, 2, rows, n_dp, hidden_rows)
    both_grad = both_grad.transpose(1, 2, 3, 0, 4).reshape(2, rows, hidden_units).astype(WIDE)
    gate_weight_grad, up_weight_grad = both_grad[0], both_grad[1]
    branch_part = after(branch_part, *grad_slots[1:]).reshape(2, n_ctx, rows, width)
    branch_part = branch_part.transpose(1, 0, 2, 3).reshape(n_ctx * 2 * rows, width)
    branch_grad = ctx_rows_scatter(branch_part, pair_sum).reshape(2, rows, width)
    down_sent = after(down_sent[0], pair_sum), down_sent[1]
    came = line_send(down_sent, n_ctx, n_ctx - 1)
    down_value = down_slots[0].astype(WIDE) + came[0].astype(WIDE) + came[1].astype(WIDE)
    block_output = (residual + down_value).astype(LOW)
    return (
        block_output,
        input_grad,
        pair_weight_grad[:, 2 * pair_width],
        pair_weight_grad[:, 2 * pair_width + 1],
        branch_grad[1],
        pair_weight_grad[:, :pair_width],
        pair_weight_grad[:, pair_width : 2 * pair_width],
        branch_grad[0],
        gate_weight_grad,
        up_weight_grad,
        down_weight_grad,
    )


def solution(mesh):
    n_dp, n_ctx = mesh.shape["dp"], mesh.shape["ctx"]
    n_core = 2 if n_dp % 2 == 0 else 1
    n_chips = n_dp // n_core
    n_y = math.isqrt(n_chips)
    while n_chips % n_y:
        n_y -= 1
    axes = ("y", "x", "core", "ctx")
    fine = Mesh(mesh.devices.reshape(n_y, n_chips // n_y, n_core, n_ctx), axes)
    matrix = P(axes, None)
    vector = P(axes)
    per_sequence = P(PLANES, None)
    return jax.shard_map(
        per_device,
        mesh=fine,
        in_specs=(matrix, matrix, per_sequence, per_sequence, vector, vector) + (matrix,) * 7,
        out_specs=(matrix, matrix, vector, vector) + (matrix,) * 7,
        check_vma=False,
    )
```

```python
import math

import jax
import jax.numpy as jnp
from jax import lax
from jax.experimental import pallas as pl
from jax.experimental.pallas import tpu as pltpu
from jax.sharding import Mesh
from jax.sharding import PartitionSpec as P

HEAD_DIM = 64
EPSILON = 1e-05
ROPE_BASE = 500000.0
MASKED_SCORE = -1e30
LANES = 128
GROUP = 4
SCORE_SCALE = HEAD_DIM**-0.5
KERNEL_MEMORY = 40 * 2**20
FEED_MEMORY = 56 * 2**20
FEED_STEP = 256
BACK_COST = pl.CostEstimate(flops=24_000_000_000, bytes_accessed=10_000_000, transcendentals=0)
COST = pl.CostEstimate(flops=1_000_000, bytes_accessed=1_000_000, transcendentals=0)

LOW = jnp.bfloat16
WIDE = jnp.float32
NN = (((1,), (0,)), ((), ()))
NT = (((1,), (1,)), ((), ()))
TN = (((0,), (0,)), ((), ()))


def dot(left, right, dims):
    return lax.dot_general(left, right, dims, preferred_element_type=WIDE)


def inverse_root(values):
    return lax.rsqrt(jnp.mean(values * values, axis=-1, keepdims=True) + EPSILON)


def norm_back(values, grad_normed):
    scaled = inverse_root(values)
    unit_rows = values * scaled
    return scaled * (
        grad_normed - unit_rows * jnp.mean(grad_normed * unit_rows, axis=-1, keepdims=True)
    )


def tie_kernel(*refs):
    del refs


def after(values, *earlier):
    anywhere = pl.BlockSpec(memory_space=pl.ANY)
    return pl.pallas_call(
        tie_kernel,
        in_specs=[anywhere] * (1 + len(earlier)),
        out_specs=anywhere,
        out_shape=jax.ShapeDtypeStruct(values.shape, values.dtype),
        input_output_aliases={0: 0},
        name="after",
    )(values, *earlier)


def turned(values, cosine, sine, first_half):
    ahead = pltpu.roll(values, LANES - HEAD_DIM // 2, 1)
    behind = pltpu.roll(values, HEAD_DIM // 2, 1)
    return values * cosine + jnp.where(first_half, ahead, behind) * sine


def lane_index():
    return lax.broadcasted_iota(jnp.int32, (1, LANES), 1)


def first_half_lanes():
    return lax.rem(lane_index(), HEAD_DIM) < HEAD_DIM // 2


def placed(block, member, head):
    start = member * GROUP * HEAD_DIM + (head // 2) * LANES
    values = block[:, start : start + LANES]
    if head % 2 != member:
        values = pltpu.roll(values, HEAD_DIM, 1)
    own = (lane_index() >= HEAD_DIM) if member else (lane_index() < HEAD_DIM)
    return jnp.where(own, values, jnp.zeros_like(values))


def forward_kernel(
    raw_ref, cos_ref, sin_ref, key_ref, value_ref, bias_ref, query_ref, out_ref, log_ref
):
    half = first_half_lanes()
    cosine, sine = cos_ref[...], sin_ref[...]
    wide = raw_ref.shape[1]
    block = jnp.concatenate(
        [
            turned(raw_ref[:, c : c + LANES], cosine, sine, half).astype(LOW).astype(WIDE)
            * SCORE_SCALE
            for c in range(0, wide, LANES)
        ],
        1,
    )
    query_ref[...] = block.astype(LOW)
    keys, values = key_ref[...], value_ref[...]
    span = GROUP * HEAD_DIM
    for member in range(2):
        parts = []
        for head in range(GROUP):
            query = placed(block, member, head).astype(LOW)
            scores = dot(keys, query, NT) + bias_ref[...]
            top = jnp.max(scores, 0, keepdims=True)
            exponent = jnp.exp(scores - top)
            total = jnp.sum(exponent, 0, keepdims=True)
            mixed = dot(values, exponent.astype(LOW), TN)
            parts.append(mixed[member * HEAD_DIM : (member + 1) * HEAD_DIM] / total)
            row = member * GROUP + head
            log_ref[row : row + 1, :] = top + jnp.log(total)
        out_ref[:, member * span : (member + 1) * span] = jnp.concatenate(parts, 0).T.astype(LOW)


def backward_kernel(
    query_ref,
    cos_ref,
    sin_ref,
    key_ref,
    value_ref,
    bias_ref,
    grad_ref,
    out_ref,
    log_ref,
    grad_query_ref,
    grad_key_ref,
    grad_value_ref,
):
    half = first_half_lanes()
    cosine, sine = cos_ref[...], -sin_ref[...]
    block = query_ref[...].astype(WIDE)
    grad = grad_ref[...].astype(WIDE)
    product = grad * out_ref[...].astype(WIDE)
    keys, values = key_ref[...], value_ref[...]
    span = GROUP * HEAD_DIM
    grad_keys = grad_values = None
    for member in range(2):
        parts = []
        product_t = product[:, member * span : (member + 1) * span].T
        for head in range(GROUP):
            query = placed(block, member, head).astype(LOW)
            grad_out = placed(grad, member, head).astype(LOW)
            row = member * GROUP + head
            delta = jnp.sum(
                product_t[head * HEAD_DIM : (head + 1) * HEAD_DIM], 0, keepdims=True
            )
            scores = dot(keys, query, NT) + bias_ref[...]
            probs = jnp.exp(scores - log_ref[row : row + 1, :])
            grad_probs = dot(values, grad_out, NT)
            grad_scores = (probs * (grad_probs - delta)).astype(LOW)
            key_part = dot(grad_scores, query, NN)
            value_part = dot(probs.astype(LOW), grad_out, NN)
            grad_keys = key_part if grad_keys is None else grad_keys + key_part
            grad_values = value_part if grad_values is None else grad_values + value_part
            query_part = dot(keys, grad_scores, TN)
            parts.append(query_part[member * HEAD_DIM : (member + 1) * HEAD_DIM] * SCORE_SCALE)
        grad_query = jnp.concatenate(parts, 0).T
        for c in range(0, span, LANES):
            grad_query_ref[:, member * span + c : member * span + c + LANES] = turned(
                grad_query[:, c : c + LANES], cosine, sine, half
            ).astype(LOW)
    grad_key_ref[...] = grad_keys.astype(LOW)
    grad_value_ref[...] = grad_values.astype(LOW)


def turn_kernel(values_ref, cos_ref, sin_ref, out_ref):
    half = first_half_lanes()
    width = values_ref.shape[1]
    for c in range(0, width // 2, LANES):
        out_ref[:, c : c + LANES] = turned(
            values_ref[:, c : c + LANES], cos_ref[...], sin_ref[...], half
        ).astype(LOW)
    out_ref[:, width // 2 :] = values_ref[:, width // 2 :].astype(LOW)


def feed_kernel(
    token_ref, goal_ref, gate_ref, up_ref, down_ref, active_ref, grad_gate_ref, grad_up_ref
):
    gate, up = dot(token_ref[...], gate_ref[...], NN), dot(token_ref[...], up_ref[...], NN)
    grad_active = dot(goal_ref[...], down_ref[...], NT)
    sigmoid = 1.0 / (1.0 + jnp.exp(-gate))
    silu = gate * sigmoid
    active_ref[...] = (silu * up).astype(LOW)
    grad_gate_ref[...] = (grad_active * up * sigmoid * (1.0 + gate * (1.0 - sigmoid))).astype(LOW)
    grad_up_ref[...] = (grad_active * silu).astype(LOW)


def second_kernel(grad_gate_ref, grad_up_ref, gate_ref, up_ref, out_ref):
    out_ref[...] = (
        dot(grad_gate_ref[...], gate_ref[...], NT) + dot(grad_up_ref[...], up_ref[...], NT)
    ).astype(LOW)


def feed_specs(count, width):
    whole = pl.BlockSpec((count, width), lambda i: (0, 0))
    return whole, pl.BlockSpec((count, FEED_STEP), lambda i: (0, i))


def feed(tokens, goal, both, down):
    count, width = tokens.shape
    hidden = down.shape[0]
    steps = hidden // FEED_STEP
    whole, part = feed_specs(count, width)
    return pl.pallas_call(
        feed_kernel,
        grid=(steps,),
        in_specs=[
            whole,
            whole,
            pl.BlockSpec((width, FEED_STEP), lambda i: (0, i)),
            pl.BlockSpec((width, FEED_STEP), lambda i: (0, i + steps)),
            pl.BlockSpec((FEED_STEP, width), lambda i: (i, 0)),
        ],
        out_specs=[part, part, part],
        out_shape=[jax.ShapeDtypeStruct((count, hidden), LOW)] * 3,
        compiler_params=pltpu.CompilerParams(vmem_limit_bytes=FEED_MEMORY),
        cost_estimate=COST,
        name="feed",
    )(tokens, goal, both, both, down)


def feed_back(grad_gate, grad_up, both):
    count, hidden = grad_gate.shape
    width = both.shape[0]
    whole, part = feed_specs(count, hidden)
    return pl.pallas_call(
        second_kernel,
        grid=(width // FEED_STEP,),
        in_specs=[
            whole,
            whole,
            pl.BlockSpec((FEED_STEP, hidden), lambda i: (i, 0)),
            pl.BlockSpec((FEED_STEP, hidden), lambda i: (i, 1)),
        ],
        out_specs=part,
        out_shape=jax.ShapeDtypeStruct((count, width), LOW),
        compiler_params=pltpu.CompilerParams(vmem_limit_bytes=FEED_MEMORY),
        cost_estimate=COST,
        name="feed_back",
    )(grad_gate, grad_up, both, both)


def weight_kernel(shared, parts, core_ref, *refs):
    del core_ref
    sides = max(shared) + 1
    lefts, rest = refs[: sides * parts], refs[sides * parts :]
    rights, out_ref = rest[: len(shared) * parts], rest[-1]
    came_ref = rest[-2] if len(rest) > len(shared) * parts + 1 else None
    for kind, side in enumerate(shared):

        @pl.when(pl.program_id(1) == kind)
        def _():
            total = None
            for part in range(parts):
                term = dot(
                    lefts[side * parts + part][...], rights[kind * parts + part][...], TN
                )
                total = term if total is None else total + term
            if came_ref is not None:
                total = total + came_ref[...].astype(WIDE)
            out_ref[...] = total.astype(LOW)


def weight_rows(lefts, rights, shared, index, chips, n_core, came=None):
    tokens, columns = rights[0][0].shape
    kinds, parts = len(rights), len(rights[0])
    size = lefts[0][0].shape[1] // (chips * n_core)
    left = pl.BlockSpec((tokens, size), lambda i, g, core: (0, i * n_core + core[0]))
    right = pl.BlockSpec((tokens, columns), lambda i, g, core: (0, 0))
    out = pl.BlockSpec((size, columns), lambda i, g, core: (i * kinds + g, 0))
    return pl.pallas_call(
        lambda *refs: weight_kernel(shared, parts, *refs),
        grid_spec=pltpu.PrefetchScalarGridSpec(
            num_scalar_prefetch=1,
            grid=(chips, kinds),
            in_specs=[left] * (parts * len(lefts))
            + [right] * (kinds * parts)
            + ([] if came is None else [out]),
            out_specs=out,
        ),
        out_shape=jax.ShapeDtypeStruct((chips * kinds * size, columns), LOW),
        compiler_params=pltpu.CompilerParams(vmem_limit_bytes=FEED_MEMORY),
        cost_estimate=pl.CostEstimate(
            flops=2 * chips * kinds * size * columns * tokens * parts,
            bytes_accessed=2 * chips * kinds * size * columns,
            transcendentals=0,
        ),
        name="weight_rows",
    )(
        jnp.reshape(index, (1,)).astype(jnp.int32),
        *(part for side in lefts for part in side),
        *(part for kind in rights for part in kind),
        *([] if came is None else [came]),
    )


def fixed_block(shape):
    return pl.BlockSpec(shape, lambda i: (0, 0))


def attention_blocks(count, length, steps):
    span = 2 * GROUP * HEAD_DIM
    return (
        pl.BlockSpec((count, span), lambda i: (0, i)),
        pl.BlockSpec((length, LANES), lambda i: (0, i)),
        pl.BlockSpec((length, LANES), lambda i: (0, i + steps)),
        pl.BlockSpec((2 * GROUP, count), lambda i: (i, 0)),
    )


def attend(raw, cosine, sine, pair, bias):
    count, length = raw.shape[0], pair.shape[0]
    steps = pair.shape[1] // 2 // LANES
    wide, key, value, rows = attention_blocks(count, length, steps)
    table = fixed_block((count, LANES))
    return pl.pallas_call(
        forward_kernel,
        grid=(steps,),
        in_specs=[wide, table, table, key, value, fixed_block((length, count))],
        out_specs=[wide, wide, rows],
        out_shape=[
            jax.ShapeDtypeStruct(raw.shape, LOW),
            jax.ShapeDtypeStruct(raw.shape, LOW),
            jax.ShapeDtypeStruct((steps * 2 * GROUP, count), WIDE),
        ],
        compiler_params=pltpu.CompilerParams(vmem_limit_bytes=KERNEL_MEMORY),
        cost_estimate=COST,
        name="attend",
    )(raw, cosine, sine, pair, pair, bias)


def attend_back(query, cosine, sine, pair, bias, grad, out, log_total):
    count, length = query.shape[0], pair.shape[0]
    steps = pair.shape[1] // 2 // LANES
    wide, key, value, rows = attention_blocks(count, length, steps)
    table = fixed_block((count, LANES))
    half = jax.ShapeDtypeStruct((length, steps * LANES), LOW)
    return pl.pallas_call(
        backward_kernel,
        grid=(steps,),
        in_specs=[wide, table, table, key, value, fixed_block((length, count)), wide, wide, rows],
        out_specs=[wide, key, key],
        out_shape=[jax.ShapeDtypeStruct(query.shape, LOW), half, half],
        compiler_params=pltpu.CompilerParams(vmem_limit_bytes=KERNEL_MEMORY),
        cost_estimate=BACK_COST,
        name="attend_back",
    )(query, cosine, sine, pair, pair, bias, grad, out, log_total)


def turn_pair(values, cosine, sine):
    return pl.pallas_call(
        turn_kernel, out_shape=jax.ShapeDtypeStruct(values.shape, LOW), name="turn_pair"
    )(values, cosine, sine)


def shift(values, count, step, senders):
    pairs = [(i, i + step) for i in senders if 0 <= i + step < count]
    return lax.ppermute(values, "ctx", pairs)


def rotate(values, count, step):
    return lax.ppermute(values, "ctx", [(i, (i + step) % count) for i in range(count)])


def line_slot(up, down, count, me, r):
    return up[0] if r == 0 else jnp.where(me >= r, up[r], down[count - r])


def line_chains(own, count):
    up, down = [own], [own]
    for s in range(1, count):
        up.append(shift(up[-1], count, 1, range(s - 1, count)))
        down.append(shift(down[-1], count, -1, range(0, count - s + 1)))
    return up, down


def line_groups(count):
    first = [r for r in range(count) if r == 0 or max(r, count - r) < count - 1]
    groups = [first, [r for r in range(count) if r not in first]]
    return [group for group in groups if group]


def line_step(slots, count, step, came):
    up, down = slots[step], slots[count - step]
    if came is not None:
        up = (up.astype(WIDE) + came[0].astype(WIDE)).astype(LOW)
        down = (down.astype(WIDE) + came[1].astype(WIDE)).astype(LOW)
    return up, down


def line_send(pair, count, step):
    up = shift(pair[0], count, 1, range(0, step))
    return up, shift(pair[1], count, -1, range(count - step, count))


def line_gather_up(own, count):
    return [own] + [shift(own, count, s, range(count)) for s in range(1, count)]


def in_order(slots, count, me):
    out = jnp.zeros((count, *slots[0].shape), slots[0].dtype)
    for r in range(count):
        out = lax.dynamic_update_index_in_dim(out, slots[r], lax.rem(me - r + count, count), 0)
    return out


CHIPS = ("y", "x")
PLANES = ("y", "x", "core")
SWAP = [(0, 1), (1, 0)]


def pick(values, index, axis):
    return lax.dynamic_index_in_dim(values, index, axis, keepdims=False)


def small_square():
    return lax.axis_size("y") == 2 and lax.axis_size("x") == 2 and lax.axis_size("core") == 2


def plane_gather(values):
    return lax.all_gather(values, PLANES, axis=0, tiled=True)


def core_columns(values, index):
    n_core, chips = lax.axis_size("core"), lax.axis_size(CHIPS)
    size = values.shape[1] // (chips * n_core)
    return jnp.concatenate(
        [
            lax.dynamic_slice_in_dim(values, (chip * n_core + index) * size, size, 1)
            for chip in range(chips)
        ],
        1,
    )


def core_term(left, right):
    if lax.axis_size("core") == 1:
        return None
    return dot(core_columns(left, 1 - lax.axis_index("core")), right, TN).astype(LOW)


def core_summed(left, right, sent=None):
    if lax.axis_size("core") == 1:
        return dot(left, right, TN).astype(LOW)
    sent = core_term(left, right) if sent is None else sent
    came = lax.ppermute(sent, "core", SWAP)
    own = core_columns(left, lax.axis_index("core"))
    return (dot(own, right, TN) + came.astype(WIDE)).astype(LOW)


def group_terms(lefts, rights, shared):
    n_core, chips = lax.axis_size("core"), lax.axis_size(CHIPS)
    core = lax.axis_index("core")
    size = lefts[0][0].shape[1] // (chips * n_core)
    if n_core == 2 and size % LANES == 0:
        sent = weight_rows(lefts, rights, shared, 1 - core, chips, n_core)

        def summed(tied, last=()):
            came = lax.ppermute(after(sent, *tied), "core", SWAP)
            came = after(came, *last) if last else came
            return weight_rows(lefts, rights, shared, core, chips, n_core, came)

        return sent, summed
    each = [
        core_summed(jnp.concatenate(lefts[side], 0), jnp.concatenate(kind, 0))
        for kind, side in zip(rights, shared)
    ]
    each = jnp.concatenate([values.reshape(chips, 1, size, -1) for values in each], 1)
    each = each.reshape(chips * len(rights) * size, -1)
    return each, lambda tied, last=(): each


def chip_scatter(values):
    return lax.psum_scatter(values, CHIPS, scatter_dimension=0, tiled=True)


def chip_scatter_steps(values, *between):
    if not small_square():
        return chip_scatter(values)
    columns = values.shape[1]
    y, x = lax.axis_index("y"), lax.axis_index("x")
    parts = values.reshape(2, 2, -1, columns)
    half = parts.shape[2] // 2
    add = lambda a, b: (a.astype(WIDE) + b.astype(WIDE)).astype(LOW)
    top, bottom = parts[:, :, :half], parts[:, :, half:]
    top_came = lax.ppermute(pick(top, 1 - x, 1), "x", SWAP)
    bottom_came = lax.ppermute(pick(bottom, 1 - y, 0), "y", SWAP)
    top = after(add(pick(top, x, 1), top_came), *between)
    bottom = add(pick(bottom, y, 0), bottom_came)
    top_came = lax.ppermute(pick(top, 1 - y, 0), "y", SWAP)
    bottom_came = lax.ppermute(pick(bottom, 1 - x, 0), "x", SWAP)
    top = add(pick(top, y, 0), top_came)
    bottom = add(pick(bottom, x, 0), bottom_came)
    return jnp.concatenate([top, bottom], 0)


def per_device(
    inputs,
    cotangent,
    segment_ids,
    real_entry_flags,
    attention_gain,
    feedforward_gain,
    query_weight,
    key_weight,
    value_weight,
    output_weight,
    gate_weight,
    up_weight,
    down_weight,
):
    n_ctx = lax.axis_size("ctx")
    n_dp = lax.axis_size(PLANES)
    me = lax.axis_index("ctx")
    entry_count, width = inputs.shape
    query_width = query_weight.shape[1]
    pair_width = key_weight.shape[1]
    hidden_units = gate_weight.shape[1]
    rows = gate_weight.shape[0]
    hidden_rows = down_weight.shape[0]
    hidden_chunk = hidden_units // n_ctx

    def ctx_rows_gather(values):
        slots = [values] + [rotate(values, n_ctx, r) for r in range(1, n_ctx)]
        return in_order(slots, n_ctx, me).reshape(n_ctx * rows, -1)

    gains = jnp.pad(
        jnp.stack([attention_gain, feedforward_gain], 1), ((0, 0), (0, LANES - 2))
    )
    pair_low = jnp.concatenate([key_weight, value_weight, gains], 1).astype(LOW)
    pair_rows = ctx_rows_gather(pair_low)
    pair_full = plane_gather(pair_rows)

    branch_low = jnp.concatenate([query_weight, output_weight], 1).astype(LOW)
    branch_rows = ctx_rows_gather(after(branch_low, pair_rows))
    branch_full = plane_gather(branch_rows)

    both = jnp.stack([gate_weight, up_weight], 1).astype(LOW)
    both = both.reshape(rows, 2, n_dp, n_ctx, hidden_rows)
    chunk_for = lambda place: pick(both, place, 3).reshape(rows, 2 * hidden_chunk)

    gain_first = pair_full[:, 2 * pair_width].astype(WIDE)
    gain_second = pair_full[:, 2 * pair_width + 1].astype(WIDE)
    pair_weight = pair_full[:, : 2 * pair_width]
    query_full = branch_full[:, :query_width]
    output_full = branch_full[:, query_width:]

    spans = segment_ids[0]
    reality = real_entry_flags[0]
    opening = me * entry_count
    places = opening + jnp.arange(entry_count, dtype=jnp.int32)
    own_spans = lax.dynamic_slice_in_dim(spans, opening, entry_count)
    doc_starts = jnp.sum((spans[None, :] < own_spans[:, None]).astype(jnp.int32), axis=1)
    offsets = (places - doc_starts).astype(WIDE)
    frequency = ROPE_BASE ** (
        -(jnp.arange(HEAD_DIM // 2, dtype=WIDE) * 2.0 / HEAD_DIM)
    )
    angle = offsets[:, None] * frequency[None, :]
    cosine, sine = jnp.cos(angle), jnp.sin(angle)
    cosine = jnp.concatenate([cosine] * 4, 1)
    sine = jnp.concatenate([-sine, sine] * 2, 1)
    key_places, key_spans, key_reality = [], [], []
    for r in range(n_ctx):
        start = (me - r) * entry_count
        key_places.append(start + jnp.arange(entry_count, dtype=jnp.int32))
        start = jnp.maximum(start, 0)
        key_spans.append(lax.dynamic_slice_in_dim(spans, start, entry_count))
        key_reality.append(lax.dynamic_slice_in_dim(reality, start, entry_count))
    key_places = jnp.concatenate(key_places)[:, None]
    key_spans = jnp.concatenate(key_spans)[:, None]
    key_reality = jnp.concatenate(key_reality)[:, None]
    allowed = (
        (own_spans[None, :] == key_spans)
        & (key_places <= places[None, :])
        & (key_places >= 0)
        & (key_reality == 1)
    ) | (key_places == places[None, :])
    bias = jnp.where(allowed, 0.0, MASKED_SCORE).astype(WIDE)

    tokens_wide = inputs.astype(WIDE)
    unit_first = tokens_wide * inverse_root(tokens_wide)
    first_hidden = (unit_first * gain_first).astype(LOW)
    both_slots = [chunk_for(me)] + [
        rotate(after(chunk_for(lax.rem(me + r, n_ctx)), branch_rows), n_ctx, r)
        for r in range(1, n_ctx)
    ]
    both_rows = in_order(both_slots, n_ctx, me).reshape(n_ctx * rows, 2 * hidden_chunk)
    both_full = plane_gather(both_rows)
    down_full = plane_gather(after(down_weight.astype(LOW), branch_rows))
    pair_own = turn_pair(dot(first_hidden, pair_weight, NN), cosine, sine)
    pair_all = jnp.concatenate(line_gather_up(after(pair_own, both_rows), n_ctx), 0)
    cot_sent = after(cotangent, pair_all)
    cot_slots = [cotangent] + [rotate(cot_sent, n_ctx, r) for r in range(1, n_ctx)]
    raw_query = dot(first_hidden, query_full, NN)
    query, attended, log_total = attend(raw_query, cosine, sine, pair_all, bias)

    residual = tokens_wide + dot(attended, output_full, NN)
    unit_second = residual * inverse_root(residual)
    second_hidden = (unit_second * gain_second).astype(LOW)
    up_chain, down_chain = line_chains(after(second_hidden, *cot_slots[1:]), n_ctx)
    groups = line_groups(n_ctx)
    hidden, cot, active, gates, ups = [], [], [], [], []
    second_slots, down_slots = [None] * n_ctx, [None] * n_ctx
    for group in groups:
        tokens = jnp.concatenate(
            [line_slot(up_chain, down_chain, n_ctx, me, r) for r in group], 0
        )
        goal = jnp.concatenate([cot_slots[r] for r in group], 0)
        if active:
            goal = after(goal, active[-1])
        group_active, grad_gate, grad_up = feed(tokens, goal, both_full, down_full)
        for kept, value in zip(
            (hidden, cot, active, gates, ups), (tokens, goal, group_active, grad_gate, grad_up)
        ):
            kept.append(value)

    second = ()
    for k in reversed(range(len(groups))):
        if k < len(groups) - 1:
            ups[k] = after(ups[k], second)
        second = feed_back(gates[k], ups[k], both_full)
        for i, r in enumerate(groups[k]):
            second_slots[r] = second[i * entry_count : (i + 1) * entry_count]

    def down_terms(k, *tied):
        if tied:
            active[k] = after(active[k], *tied)
        down_out = dot(active[k], down_full, NN).astype(LOW)
        for i, r in enumerate(groups[k]):
            down_slots[r] = down_out[i * entry_count : (i + 1) * entry_count]
        return down_out

    first = line_step(second_slots, n_ctx, 1, None)
    came, steps = line_send(first, n_ctx, 1), [first]
    early = down_terms(-1, *first)
    for step in range(2, n_ctx):
        sent = line_step(second_slots, n_ctx, step, came)
        if step == 2:
            sent = after(sent[0], early), sent[1]
        steps.append(sent)
        came = line_send(sent, n_ctx, step)
    gates[0] = after(gates[0], *steps[min(1, n_ctx - 2)])
    feed_sent, feed_summed = group_terms([hidden, active], [gates, ups, cot], [0, 0, 1])
    if len(groups) > 1:
        late = down_terms(0)
        came = after(came[0], late), came[1]
    grad_second = second_slots[0].astype(WIDE) + came[0].astype(WIDE) + came[1].astype(WIDE)
    down_sent = tuple(
        after(values, grad_second) for values in line_step(down_slots, n_ctx, 1, None)
    )
    feed_part = feed_summed(steps[-1], down_sent)
    in_slots = lambda values: [
        values[r * entry_count : (r + 1) * entry_count] for r in range(n_ctx)
    ]
    feed_rows = chip_scatter(feed_part).reshape(3, n_ctx * rows, hidden_chunk)
    both_grad_rows = feed_rows[:2]
    down_weight_grad = feed_rows[2].astype(WIDE)

    both_grad_parts = both_grad_rows.reshape(2, n_ctx, rows, hidden_chunk)
    part_for = lambda place: pick(both_grad_parts, place, 1).reshape(2 * rows, hidden_chunk)
    grad_slots = [part_for(me)] + [
        rotate(part_for(lax.rem(me + r, n_ctx)), n_ctx, r) for r in range(1, n_ctx)
    ]

    second_gain_term = jnp.sum(grad_second * unit_second, axis=0)
    grad_residual = cotangent.astype(WIDE) + norm_back(residual, grad_second * gain_second)
    grad_branch = grad_residual.astype(LOW)
    grad_attended = after(dot(grad_branch, output_full, NT).astype(LOW), feed_part)
    down_came = None
    for step in range(1, n_ctx - 1):
        if step > 1:
            down_sent = line_step(down_slots, n_ctx, step, down_came)
            grad_attended = after(grad_attended, *down_sent)
        down_came = line_send(down_sent, n_ctx, step)
    grad_query, key_part, value_part = attend_back(
        query, cosine, sine, pair_all, bias, grad_attended, attended, log_total
    )
    pair_part = jnp.concatenate([key_part, value_part], 1)
    pair_part = jnp.concatenate([key_part, value_part], 1)
    if down_came is not None:
        down_came = tuple(after(values, grad_query) for values in down_came)
        down_sent = line_step(down_slots, n_ctx, n_ctx - 1, down_came)
    pair_part = after(pair_part, *down_sent)
    pair_slots = in_slots(pair_part)
    came, steps = None, []
    for step in range(1, n_ctx):
        sent = pair_slots[n_ctx - step]
        if came is not None:
            sent = (sent.astype(WIDE) + came.astype(WIDE)).astype(LOW)
        steps.append(sent)
        came = shift(sent, n_ctx, -1, range(n_ctx - step, n_ctx))
    pair_grad = pair_slots[0].astype(WIDE) + came.astype(WIDE)
    _, branch_summed = group_terms(
        [[attended], [first_hidden]],
        [[after(grad_branch, steps[min(1, n_ctx - 2)])], [grad_query]],
        [0, 1],
    )
    branch_terms = branch_summed([steps[-1]])
    grad_pair = turn_pair(after(pair_grad, grad_slots[1]), cosine, -sine)
    grad_first = dot(grad_query, query_full, NT) + dot(grad_pair, pair_weight, NT)
    first_gain_term = jnp.sum(grad_first * unit_first, axis=0)
    input_grad = (grad_residual + norm_back(tokens_wide, grad_first * gain_first)).astype(LOW)

    def ctx_rows_scatter(values, *earlier):
        parts = values.reshape(n_ctx, -1, values.shape[1])
        own = pick(parts, me, 0)
        came = [rotate(pick(parts, lax.rem(me + r, n_ctx), 0), n_ctx, r) for r in range(1, n_ctx)]
        return [own] + [after(values, *earlier) for values in came]

    branch_part = chip_scatter(branch_terms)
    gain_terms = jnp.pad(
        jnp.stack([first_gain_term, second_gain_term], 1), ((0, 0), (0, LANES - 2))
    ).astype(LOW)
    gain_parts = gain_terms.reshape(lax.axis_size(CHIPS), lax.axis_size("core"), -1, LANES)
    gain_part = pick(gain_parts, lax.axis_index("core"), 1)
    if lax.axis_size("core") == 2:
        gain_came = lax.ppermute(pick(gain_parts, 1 - lax.axis_index("core"), 1), "core", SWAP)
        gain_part = (gain_part.astype(WIDE) + gain_came.astype(WIDE)).astype(LOW)
    pair_terms = jnp.concatenate(
        [core_summed(first_hidden, grad_pair), gain_part.reshape(-1, LANES)], 1
    )
    pair_sum = chip_scatter_steps(pair_terms, *grad_slots[1:])
    branch_part = after(branch_part, pair_sum, *grad_slots[1:]).reshape(2, n_ctx, rows, width)
    branch_part = branch_part.transpose(1, 0, 2, 3).reshape(n_ctx * 2 * rows, width)
    total = lambda parts: sum(part.astype(WIDE) for part in parts)
    arrived = ctx_rows_scatter(branch_part, pair_sum)
    pair_weight_grad = total(ctx_rows_scatter(pair_sum, arrived[1]))
    grad_slots[0] = after(grad_slots[0], arrived[1])
    both_grad = in_order(grad_slots, n_ctx, me).reshape(n_ctx, 2, rows, n_dp, hidden_rows)
    both_grad = both_grad.transpose(1, 2, 3, 0, 4).reshape(2, rows, hidden_units).astype(WIDE)
    gate_weight_grad, up_weight_grad = both_grad[0], both_grad[1]
    arrived[2:] = [after(values, gate_weight_grad) for values in arrived[2:]]
    branch_grad = total(arrived).reshape(2, rows, width)
    down_sent = after(down_sent[0], pair_terms), down_sent[1]
    came = line_send(down_sent, n_ctx, n_ctx - 1)
    down_value = down_slots[0].astype(WIDE) + came[0].astype(WIDE) + came[1].astype(WIDE)
    block_output = (residual + down_value).astype(LOW)
    return (
        block_output,
        input_grad,
        pair_weight_grad[:, 2 * pair_width],
        pair_weight_grad[:, 2 * pair_width + 1],
        branch_grad[1],
        pair_weight_grad[:, :pair_width],
        pair_weight_grad[:, pair_width : 2 * pair_width],
        branch_grad[0],
        gate_weight_grad,
        up_weight_grad,
        down_weight_grad,
    )


def solution(mesh):
    n_dp, n_ctx = mesh.shape["dp"], mesh.shape["ctx"]
    n_core = 2 if n_dp % 2 == 0 else 1
    n_chips = n_dp // n_core
    n_y = math.isqrt(n_chips)
    while n_chips % n_y:
        n_y -= 1
    axes = ("y", "x", "core", "ctx")
    fine = Mesh(mesh.devices.reshape(n_y, n_chips // n_y, n_core, n_ctx), axes)
    matrix = P(axes, None)
    vector = P(axes)
    per_sequence = P(PLANES, None)
    return jax.shard_map(
        per_device,
        mesh=fine,
        in_specs=(matrix, matrix, per_sequence, per_sequence, vector, vector) + (matrix,) * 7,
        out_specs=(matrix, matrix, vector, vector) + (matrix,) * 7,
        check_vma=False,
    )
```

```python
import math

import jax
import jax.numpy as jnp
from jax import lax
from jax.experimental import pallas as pl
from jax.experimental.pallas import tpu as pltpu
from jax.sharding import Mesh
from jax.sharding import PartitionSpec as P

HEAD_DIM = 64
EPSILON = 1e-05
ROPE_BASE = 500000.0
MASKED_SCORE = -1e30
LANES = 128
GROUP = 4
SCORE_SCALE = HEAD_DIM**-0.5
KERNEL_MEMORY = 40 * 2**20
FEED_MEMORY = 56 * 2**20
FEED_STEP = 256
BACK_COST = pl.CostEstimate(flops=24_000_000_000, bytes_accessed=10_000_000, transcendentals=0)
COST = pl.CostEstimate(flops=1_000_000, bytes_accessed=1_000_000, transcendentals=0)

LOW = jnp.bfloat16
WIDE = jnp.float32
NN = (((1,), (0,)), ((), ()))
NT = (((1,), (1,)), ((), ()))
TN = (((0,), (0,)), ((), ()))


def dot(left, right, dims):
    return lax.dot_general(left, right, dims, preferred_element_type=WIDE)


def inverse_root(values):
    return lax.rsqrt(jnp.mean(values * values, axis=-1, keepdims=True) + EPSILON)


def norm_back(values, grad_normed):
    scaled = inverse_root(values)
    unit_rows = values * scaled
    return scaled * (
        grad_normed - unit_rows * jnp.mean(grad_normed * unit_rows, axis=-1, keepdims=True)
    )


def tie_kernel(*refs):
    del refs


def after(values, *earlier):
    anywhere = pl.BlockSpec(memory_space=pl.ANY)
    return pl.pallas_call(
        tie_kernel,
        in_specs=[anywhere] * (1 + len(earlier)),
        out_specs=anywhere,
        out_shape=jax.ShapeDtypeStruct(values.shape, values.dtype),
        input_output_aliases={0: 0},
        name="after",
    )(values, *earlier)


def turned(values, cosine, sine, first_half):
    ahead = pltpu.roll(values, LANES - HEAD_DIM // 2, 1)
    behind = pltpu.roll(values, HEAD_DIM // 2, 1)
    return values * cosine + jnp.where(first_half, ahead, behind) * sine


def lane_index():
    return lax.broadcasted_iota(jnp.int32, (1, LANES), 1)


def first_half_lanes():
    return lax.rem(lane_index(), HEAD_DIM) < HEAD_DIM // 2


def placed(block, member, head):
    start = member * GROUP * HEAD_DIM + (head // 2) * LANES
    values = block[:, start : start + LANES]
    if head % 2 != member:
        values = pltpu.roll(values, HEAD_DIM, 1)
    own = (lane_index() >= HEAD_DIM) if member else (lane_index() < HEAD_DIM)
    return jnp.where(own, values, jnp.zeros_like(values))


def forward_kernel(
    raw_ref, cos_ref, sin_ref, key_ref, value_ref, bias_ref, query_ref, out_ref, log_ref
):
    half = first_half_lanes()
    cosine, sine = cos_ref[...], sin_ref[...]
    wide = raw_ref.shape[1]
    block = jnp.concatenate(
        [
            turned(raw_ref[:, c : c + LANES], cosine, sine, half).astype(LOW).astype(WIDE)
            * SCORE_SCALE
            for c in range(0, wide, LANES)
        ],
        1,
    )
    query_ref[...] = block.astype(LOW)
    keys, values = key_ref[...], value_ref[...]
    span = GROUP * HEAD_DIM
    for member in range(2):
        parts = []
        for head in range(GROUP):
            query = placed(block, member, head).astype(LOW)
            scores = dot(keys, query, NT) + bias_ref[...]
            top = jnp.max(scores, 0, keepdims=True)
            exponent = jnp.exp(scores - top)
            total = jnp.sum(exponent, 0, keepdims=True)
            mixed = dot(values, exponent.astype(LOW), TN)
            parts.append(mixed[member * HEAD_DIM : (member + 1) * HEAD_DIM] / total)
            row = member * GROUP + head
            log_ref[row : row + 1, :] = top + jnp.log(total)
        out_ref[:, member * span : (member + 1) * span] = jnp.concatenate(parts, 0).T.astype(LOW)


def backward_kernel(
    query_ref,
    cos_ref,
    sin_ref,
    key_ref,
    value_ref,
    bias_ref,
    grad_ref,
    out_ref,
    log_ref,
    grad_query_ref,
    grad_key_ref,
    grad_value_ref,
):
    half = first_half_lanes()
    cosine, sine = cos_ref[...], -sin_ref[...]
    block = query_ref[...].astype(WIDE)
    grad = grad_ref[...].astype(WIDE)
    product = grad * out_ref[...].astype(WIDE)
    keys, values = key_ref[...], value_ref[...]
    span = GROUP * HEAD_DIM
    grad_keys = grad_values = None
    for member in range(2):
        parts = []
        product_t = product[:, member * span : (member + 1) * span].T
        for head in range(GROUP):
            query = placed(block, member, head).astype(LOW)
            grad_out = placed(grad, member, head).astype(LOW)
            row = member * GROUP + head
            delta = jnp.sum(
                product_t[head * HEAD_DIM : (head + 1) * HEAD_DIM], 0, keepdims=True
            )
            scores = dot(keys, query, NT) + bias_ref[...]
            probs = jnp.exp(scores - log_ref[row : row + 1, :])
            grad_probs = dot(values, grad_out, NT)
            grad_scores = (probs * (grad_probs - delta)).astype(LOW)
            key_part = dot(grad_scores, query, NN)
            value_part = dot(probs.astype(LOW), grad_out, NN)
            grad_keys = key_part if grad_keys is None else grad_keys + key_part
            grad_values = value_part if grad_values is None else grad_values + value_part
            query_part = dot(keys, grad_scores, TN)
            parts.append(query_part[member * HEAD_DIM : (member + 1) * HEAD_DIM] * SCORE_SCALE)
        grad_query = jnp.concatenate(parts, 0).T
        for c in range(0, span, LANES):
            grad_query_ref[:, member * span + c : member * span + c + LANES] = turned(
                grad_query[:, c : c + LANES], cosine, sine, half
            ).astype(LOW)
    grad_key_ref[...] = grad_keys.astype(LOW)
    grad_value_ref[...] = grad_values.astype(LOW)


def turn_kernel(values_ref, cos_ref, sin_ref, out_ref):
    half = first_half_lanes()
    width = values_ref.shape[1]
    for c in range(0, width // 2, LANES):
        out_ref[:, c : c + LANES] = turned(
            values_ref[:, c : c + LANES], cos_ref[...], sin_ref[...], half
        ).astype(LOW)
    out_ref[:, width // 2 :] = values_ref[:, width // 2 :].astype(LOW)


def feed_kernel(
    token_ref, goal_ref, gate_ref, up_ref, down_ref, active_ref, grad_gate_ref, grad_up_ref
):
    gate, up = dot(token_ref[...], gate_ref[...], NN), dot(token_ref[...], up_ref[...], NN)
    grad_active = dot(goal_ref[...], down_ref[...], NT)
    sigmoid = 1.0 / (1.0 + jnp.exp(-gate))
    silu = gate * sigmoid
    active_ref[...] = (silu * up).astype(LOW)
    grad_gate_ref[...] = (grad_active * up * sigmoid * (1.0 + gate * (1.0 - sigmoid))).astype(LOW)
    grad_up_ref[...] = (grad_active * silu).astype(LOW)


def second_kernel(grad_gate_ref, grad_up_ref, gate_ref, up_ref, out_ref):
    out_ref[...] = (
        dot(grad_gate_ref[...], gate_ref[...], NT) + dot(grad_up_ref[...], up_ref[...], NT)
    ).astype(LOW)


def feed_specs(count, width):
    whole = pl.BlockSpec((count, width), lambda i: (0, 0))
    return whole, pl.BlockSpec((count, FEED_STEP), lambda i: (0, i))


def feed(tokens, goal, both, down):
    count, width = tokens.shape
    hidden = down.shape[0]
    steps = hidden // FEED_STEP
    whole, part = feed_specs(count, width)
    return pl.pallas_call(
        feed_kernel,
        grid=(steps,),
        in_specs=[
            whole,
            whole,
            pl.BlockSpec((width, FEED_STEP), lambda i: (0, i)),
            pl.BlockSpec((width, FEED_STEP), lambda i: (0, i + steps)),
            pl.BlockSpec((FEED_STEP, width), lambda i: (i, 0)),
        ],
        out_specs=[part, part, part],
        out_shape=[jax.ShapeDtypeStruct((count, hidden), LOW)] * 3,
        compiler_params=pltpu.CompilerParams(vmem_limit_bytes=FEED_MEMORY),
        cost_estimate=COST,
        name="feed",
    )(tokens, goal, both, both, down)


def feed_back(grad_gate, grad_up, both):
    count, hidden = grad_gate.shape
    width = both.shape[0]
    whole, part = feed_specs(count, hidden)
    return pl.pallas_call(
        second_kernel,
        grid=(width // FEED_STEP,),
        in_specs=[
            whole,
            whole,
            pl.BlockSpec((FEED_STEP, hidden), lambda i: (i, 0)),
            pl.BlockSpec((FEED_STEP, hidden), lambda i: (i, 1)),
        ],
        out_specs=part,
        out_shape=jax.ShapeDtypeStruct((count, width), LOW),
        compiler_params=pltpu.CompilerParams(vmem_limit_bytes=FEED_MEMORY),
        cost_estimate=COST,
        name="feed_back",
    )(grad_gate, grad_up, both, both)


def weight_kernel(shared, parts, core_ref, *refs):
    del core_ref
    sides = max(shared) + 1
    lefts, rest = refs[: sides * parts], refs[sides * parts :]
    rights, out_ref = rest[: len(shared) * parts], rest[-1]
    came_ref = rest[-2] if len(rest) > len(shared) * parts + 1 else None
    for kind, side in enumerate(shared):

        @pl.when(pl.program_id(1) == kind)
        def _():
            total = None
            for part in range(parts):
                term = dot(
                    lefts[side * parts + part][...], rights[kind * parts + part][...], TN
                )
                total = term if total is None else total + term
            if came_ref is not None:
                total = total + came_ref[...].astype(WIDE)
            out_ref[...] = total.astype(LOW)


def weight_rows(lefts, rights, shared, index, chips, n_core, came=None):
    tokens, columns = rights[0][0].shape
    kinds, parts = len(rights), len(rights[0])
    size = lefts[0][0].shape[1] // (chips * n_core)
    left = pl.BlockSpec((tokens, size), lambda i, g, core: (0, i * n_core + core[0]))
    right = pl.BlockSpec((tokens, columns), lambda i, g, core: (0, 0))
    out = pl.BlockSpec((size, columns), lambda i, g, core: (i * kinds + g, 0))
    return pl.pallas_call(
        lambda *refs: weight_kernel(shared, parts, *refs),
        grid_spec=pltpu.PrefetchScalarGridSpec(
            num_scalar_prefetch=1,
            grid=(chips, kinds),
            in_specs=[left] * (parts * len(lefts))
            + [right] * (kinds * parts)
            + ([] if came is None else [out]),
            out_specs=out,
        ),
        out_shape=jax.ShapeDtypeStruct((chips * kinds * size, columns), LOW),
        compiler_params=pltpu.CompilerParams(vmem_limit_bytes=FEED_MEMORY),
        cost_estimate=pl.CostEstimate(
            flops=2 * chips * kinds * size * columns * tokens * parts,
            bytes_accessed=2 * chips * kinds * size * columns,
            transcendentals=0,
        ),
        name="weight_rows",
    )(
        jnp.reshape(index, (1,)).astype(jnp.int32),
        *(part for side in lefts for part in side),
        *(part for kind in rights for part in kind),
        *([] if came is None else [came]),
    )


def fixed_block(shape):
    return pl.BlockSpec(shape, lambda i: (0, 0))


def attention_blocks(count, length, steps):
    span = 2 * GROUP * HEAD_DIM
    return (
        pl.BlockSpec((count, span), lambda i: (0, i)),
        pl.BlockSpec((length, LANES), lambda i: (0, i)),
        pl.BlockSpec((length, LANES), lambda i: (0, i + steps)),
        pl.BlockSpec((2 * GROUP, count), lambda i: (i, 0)),
    )


def attend(raw, cosine, sine, pair, bias):
    count, length = raw.shape[0], pair.shape[0]
    steps = pair.shape[1] // 2 // LANES
    wide, key, value, rows = attention_blocks(count, length, steps)
    table = fixed_block((count, LANES))
    return pl.pallas_call(
        forward_kernel,
        grid=(steps,),
        in_specs=[wide, table, table, key, value, fixed_block((length, count))],
        out_specs=[wide, wide, rows],
        out_shape=[
            jax.ShapeDtypeStruct(raw.shape, LOW),
            jax.ShapeDtypeStruct(raw.shape, LOW),
            jax.ShapeDtypeStruct((steps * 2 * GROUP, count), WIDE),
        ],
        compiler_params=pltpu.CompilerParams(vmem_limit_bytes=KERNEL_MEMORY),
        cost_estimate=COST,
        name="attend",
    )(raw, cosine, sine, pair, pair, bias)


def attend_back(query, cosine, sine, pair, bias, grad, out, log_total):
    count, length = query.shape[0], pair.shape[0]
    steps = pair.shape[1] // 2 // LANES
    wide, key, value, rows = attention_blocks(count, length, steps)
    table = fixed_block((count, LANES))
    half = jax.ShapeDtypeStruct((length, steps * LANES), LOW)
    return pl.pallas_call(
        backward_kernel,
        grid=(steps,),
        in_specs=[wide, table, table, key, value, fixed_block((length, count)), wide, wide, rows],
        out_specs=[wide, key, key],
        out_shape=[jax.ShapeDtypeStruct(query.shape, LOW), half, half],
        compiler_params=pltpu.CompilerParams(vmem_limit_bytes=KERNEL_MEMORY),
        cost_estimate=BACK_COST,
        name="attend_back",
    )(query, cosine, sine, pair, pair, bias, grad, out, log_total)


def turn_pair(values, cosine, sine):
    return pl.pallas_call(
        turn_kernel, out_shape=jax.ShapeDtypeStruct(values.shape, LOW), name="turn_pair"
    )(values, cosine, sine)


def spread_kernel(me_ref, *refs):
    count, out_ref = len(refs) - 1, refs[-1]
    width = refs[0].shape[1]
    for r in range(count):
        place = lax.rem(me_ref[0] - r + count, count)
        start = pl.multiple_of(place * width, LANES)
        out_ref[:, pl.ds(start, width)] = refs[r][...].astype(WIDE)


def spread(slots, me, kind, rows, blocks):
    count, width = len(slots), slots[0].shape[1] // blocks
    part = pl.BlockSpec((rows, width), lambda i, me: (kind, i))
    return pl.pallas_call(
        spread_kernel,
        grid_spec=pltpu.PrefetchScalarGridSpec(
            num_scalar_prefetch=1,
            grid=(blocks,),
            in_specs=[part] * count,
            out_specs=pl.BlockSpec((rows, count * width), lambda i, me: (0, i)),
        ),
        out_shape=jax.ShapeDtypeStruct((rows, blocks * count * width), WIDE),
        name="spread",
    )(jnp.reshape(me, (1,)).astype(jnp.int32), *slots)


def shift(values, count, step, senders):
    pairs = [(i, i + step) for i in senders if 0 <= i + step < count]
    return lax.ppermute(values, "ctx", pairs)


def rotate(values, count, step):
    return lax.ppermute(values, "ctx", [(i, (i + step) % count) for i in range(count)])


def line_slot(up, down, count, me, r):
    return up[0] if r == 0 else jnp.where(me >= r, up[r], down[count - r])


def line_chains(own, count):
    up, down = [own], [own]
    for s in range(1, count):
        up.append(shift(up[-1], count, 1, range(s - 1, count)))
        down.append(shift(down[-1], count, -1, range(0, count - s + 1)))
    return up, down


def line_groups(count):
    first = [r for r in range(count) if r == 0 or max(r, count - r) < count - 1]
    groups = [first, [r for r in range(count) if r not in first]]
    return [group for group in groups if group]


def line_step(slots, count, step, came):
    up, down = slots[step], slots[count - step]
    if came is not None:
        up = (up.astype(WIDE) + came[0].astype(WIDE)).astype(LOW)
        down = (down.astype(WIDE) + came[1].astype(WIDE)).astype(LOW)
    return up, down


def line_send(pair, count, step):
    up = shift(pair[0], count, 1, range(0, step))
    return up, shift(pair[1], count, -1, range(count - step, count))


def line_gather_up(own, count):
    return [own] + [shift(own, count, s, range(count)) for s in range(1, count)]


def in_order(slots, count, me):
    out = jnp.zeros((count, *slots[0].shape), slots[0].dtype)
    for r in range(count):
        out = lax.dynamic_update_index_in_dim(out, slots[r], lax.rem(me - r + count, count), 0)
    return out


CHIPS = ("y", "x")
PLANES = ("y", "x", "core")
SWAP = [(0, 1), (1, 0)]


def pick(values, index, axis):
    return lax.dynamic_index_in_dim(values, index, axis, keepdims=False)


def small_square():
    return lax.axis_size("y") == 2 and lax.axis_size("x") == 2 and lax.axis_size("core") == 2


def plane_gather(values):
    return lax.all_gather(values, PLANES, axis=0, tiled=True)


def core_columns(values, index):
    n_core, chips = lax.axis_size("core"), lax.axis_size(CHIPS)
    size = values.shape[1] // (chips * n_core)
    return jnp.concatenate(
        [
            lax.dynamic_slice_in_dim(values, (chip * n_core + index) * size, size, 1)
            for chip in range(chips)
        ],
        1,
    )


def core_term(left, right):
    if lax.axis_size("core") == 1:
        return None
    return dot(core_columns(left, 1 - lax.axis_index("core")), right, TN).astype(LOW)


def core_summed(left, right, sent=None):
    if lax.axis_size("core") == 1:
        return dot(left, right, TN).astype(LOW)
    sent = core_term(left, right) if sent is None else sent
    came = lax.ppermute(sent, "core", SWAP)
    own = core_columns(left, lax.axis_index("core"))
    return (dot(own, right, TN) + came.astype(WIDE)).astype(LOW)


def group_terms(lefts, rights, shared):
    n_core, chips = lax.axis_size("core"), lax.axis_size(CHIPS)
    core = lax.axis_index("core")
    size = lefts[0][0].shape[1] // (chips * n_core)
    if n_core == 2 and size % LANES == 0:
        sent = weight_rows(lefts, rights, shared, 1 - core, chips, n_core)

        def summed(tied, last=()):
            came = lax.ppermute(after(sent, *tied), "core", SWAP)
            came = after(came, *last) if last else came
            return weight_rows(lefts, rights, shared, core, chips, n_core, came)

        return sent, summed
    each = [
        core_summed(jnp.concatenate(lefts[side], 0), jnp.concatenate(kind, 0))
        for kind, side in zip(rights, shared)
    ]
    each = jnp.concatenate([values.reshape(chips, 1, size, -1) for values in each], 1)
    each = each.reshape(chips * len(rights) * size, -1)
    return each, lambda tied, last=(): each


def chip_scatter(values):
    return lax.psum_scatter(values, CHIPS, scatter_dimension=0, tiled=True)


def chip_scatter_steps(values, *between):
    if not small_square():
        return chip_scatter(values), values
    columns = values.shape[1]
    y, x = lax.axis_index("y"), lax.axis_index("x")
    parts = values.reshape(2, 2, -1, columns)
    half = parts.shape[2] // 2
    add = lambda a, b: (a.astype(WIDE) + b.astype(WIDE)).astype(LOW)
    top, bottom = parts[:, :, :half], parts[:, :, half:]
    top_came = lax.ppermute(pick(top, 1 - x, 1), "x", SWAP)
    bottom_came = lax.ppermute(pick(bottom, 1 - y, 0), "y", SWAP)
    top = after(add(pick(top, x, 1), top_came), *between)
    bottom = add(pick(bottom, y, 0), bottom_came)
    middle = pick(bottom, 1 - x, 0)
    top_came = lax.ppermute(pick(top, 1 - y, 0), "y", SWAP)
    bottom_came = lax.ppermute(middle, "x", SWAP)
    top = add(pick(top, y, 0), top_came)
    bottom = add(pick(bottom, x, 0), bottom_came)
    return jnp.concatenate([top, bottom], 0), middle


def per_device(
    inputs,
    cotangent,
    segment_ids,
    real_entry_flags,
    attention_gain,
    feedforward_gain,
    query_weight,
    key_weight,
    value_weight,
    output_weight,
    gate_weight,
    up_weight,
    down_weight,
):
    n_ctx = lax.axis_size("ctx")
    n_dp = lax.axis_size(PLANES)
    me = lax.axis_index("ctx")
    entry_count, width = inputs.shape
    query_width = query_weight.shape[1]
    pair_width = key_weight.shape[1]
    hidden_units = gate_weight.shape[1]
    rows = gate_weight.shape[0]
    hidden_rows = down_weight.shape[0]
    hidden_chunk = hidden_units // n_ctx

    def ctx_rows_gather(values):
        slots = [values] + [rotate(values, n_ctx, r) for r in range(1, n_ctx)]
        return in_order(slots, n_ctx, me).reshape(n_ctx * rows, -1)

    gains = jnp.pad(
        jnp.stack([attention_gain, feedforward_gain], 1), ((0, 0), (0, LANES - 2))
    )
    pair_low = jnp.concatenate([key_weight, value_weight, gains], 1).astype(LOW)
    pair_rows = ctx_rows_gather(pair_low)
    pair_full = plane_gather(pair_rows)

    branch_low = jnp.concatenate([query_weight, output_weight], 1).astype(LOW)
    branch_rows = ctx_rows_gather(after(branch_low, pair_rows))
    branch_full = plane_gather(branch_rows)

    both = jnp.stack([gate_weight, up_weight], 1).astype(LOW)
    both = both.reshape(rows, 2, n_dp, n_ctx, hidden_rows)
    chunk_for = lambda place: pick(both, place, 3).reshape(rows, 2 * hidden_chunk)

    gain_first = pair_full[:, 2 * pair_width].astype(WIDE)
    gain_second = pair_full[:, 2 * pair_width + 1].astype(WIDE)
    pair_weight = pair_full[:, : 2 * pair_width]
    query_full = branch_full[:, :query_width]
    output_full = branch_full[:, query_width:]

    spans = segment_ids[0]
    reality = real_entry_flags[0]
    opening = me * entry_count
    places = opening + jnp.arange(entry_count, dtype=jnp.int32)
    own_spans = lax.dynamic_slice_in_dim(spans, opening, entry_count)
    doc_starts = jnp.sum((spans[None, :] < own_spans[:, None]).astype(jnp.int32), axis=1)
    offsets = (places - doc_starts).astype(WIDE)
    frequency = ROPE_BASE ** (
        -(jnp.arange(HEAD_DIM // 2, dtype=WIDE) * 2.0 / HEAD_DIM)
    )
    angle = offsets[:, None] * frequency[None, :]
    cosine, sine = jnp.cos(angle), jnp.sin(angle)
    cosine = jnp.concatenate([cosine] * 4, 1)
    sine = jnp.concatenate([-sine, sine] * 2, 1)
    key_places, key_spans, key_reality = [], [], []
    for r in range(n_ctx):
        start = (me - r) * entry_count
        key_places.append(start + jnp.arange(entry_count, dtype=jnp.int32))
        start = jnp.maximum(start, 0)
        key_spans.append(lax.dynamic_slice_in_dim(spans, start, entry_count))
        key_reality.append(lax.dynamic_slice_in_dim(reality, start, entry_count))
    key_places = jnp.concatenate(key_places)[:, None]
    key_spans = jnp.concatenate(key_spans)[:, None]
    key_reality = jnp.concatenate(key_reality)[:, None]
    allowed = (
        (own_spans[None, :] == key_spans)
        & (key_places <= places[None, :])
        & (key_places >= 0)
        & (key_reality == 1)
    ) | (key_places == places[None, :])
    bias = jnp.where(allowed, 0.0, MASKED_SCORE).astype(WIDE)

    tokens_wide = inputs.astype(WIDE)
    unit_first = tokens_wide * inverse_root(tokens_wide)
    first_hidden = (unit_first * gain_first).astype(LOW)
    both_slots = [chunk_for(me)] + [
        rotate(after(chunk_for(lax.rem(me + r, n_ctx)), branch_rows), n_ctx, r)
        for r in range(1, n_ctx)
    ]
    both_rows = in_order(both_slots, n_ctx, me).reshape(n_ctx * rows, 2 * hidden_chunk)
    both_full = plane_gather(both_rows)
    down_full = plane_gather(after(down_weight.astype(LOW), branch_rows))
    pair_own = turn_pair(dot(first_hidden, pair_weight, NN), cosine, sine)
    pair_all = jnp.concatenate(line_gather_up(after(pair_own, both_rows), n_ctx), 0)
    cot_sent = after(cotangent, pair_all)
    cot_slots = [cotangent] + [rotate(cot_sent, n_ctx, r) for r in range(1, n_ctx)]
    raw_query = dot(first_hidden, query_full, NN)
    query, attended, log_total = attend(raw_query, cosine, sine, pair_all, bias)

    residual = tokens_wide + dot(attended, output_full, NN)
    unit_second = residual * inverse_root(residual)
    second_hidden = (unit_second * gain_second).astype(LOW)
    up_chain, down_chain = line_chains(after(second_hidden, *cot_slots[1:]), n_ctx)
    groups = line_groups(n_ctx)
    hidden, cot, active, gates, ups = [], [], [], [], []
    second_slots, down_slots = [None] * n_ctx, [None] * n_ctx
    for group in groups:
        tokens = jnp.concatenate(
            [line_slot(up_chain, down_chain, n_ctx, me, r) for r in group], 0
        )
        goal = jnp.concatenate([cot_slots[r] for r in group], 0)
        if active:
            goal = after(goal, active[-1])
        group_active, grad_gate, grad_up = feed(tokens, goal, both_full, down_full)
        for kept, value in zip(
            (hidden, cot, active, gates, ups), (tokens, goal, group_active, grad_gate, grad_up)
        ):
            kept.append(value)

    second = ()
    for k in reversed(range(len(groups))):
        if k < len(groups) - 1:
            ups[k] = after(ups[k], second)
        second = feed_back(gates[k], ups[k], both_full)
        for i, r in enumerate(groups[k]):
            second_slots[r] = second[i * entry_count : (i + 1) * entry_count]

    def down_terms(k, *tied):
        if tied:
            active[k] = after(active[k], *tied)
        down_out = dot(active[k], down_full, NN).astype(LOW)
        for i, r in enumerate(groups[k]):
            down_slots[r] = down_out[i * entry_count : (i + 1) * entry_count]
        return down_out

    first = line_step(second_slots, n_ctx, 1, None)
    came, steps = line_send(first, n_ctx, 1), [first]
    early = down_terms(-1, *first)
    for step in range(2, n_ctx):
        sent = line_step(second_slots, n_ctx, step, came)
        if step == 2:
            sent = after(sent[0], early), sent[1]
        steps.append(sent)
        came = line_send(sent, n_ctx, step)
    gates[0] = after(gates[0], *steps[min(1, n_ctx - 2)])
    feed_sent, feed_summed = group_terms([hidden, active], [gates, ups, cot], [0, 0, 1])
    if len(groups) > 1:
        late = down_terms(0)
        came = after(came[0], late), came[1]
    grad_second = second_slots[0].astype(WIDE) + came[0].astype(WIDE) + came[1].astype(WIDE)
    down_sent = tuple(
        after(values, grad_second) for values in line_step(down_slots, n_ctx, 1, None)
    )
    feed_part = feed_summed(steps[-1], down_sent)
    in_slots = lambda values: [
        values[r * entry_count : (r + 1) * entry_count] for r in range(n_ctx)
    ]
    feed_rows = chip_scatter(feed_part).reshape(3, n_ctx * rows, hidden_chunk)
    both_grad_rows = feed_rows[:2]
    down_weight_grad = feed_rows[2].astype(WIDE)

    both_grad_parts = both_grad_rows.reshape(2, n_ctx, rows, hidden_chunk)
    part_for = lambda place: pick(both_grad_parts, place, 1).reshape(2 * rows, hidden_chunk)
    grad_slots = [part_for(me)] + [
        rotate(part_for(lax.rem(me + r, n_ctx)), n_ctx, r) for r in range(1, n_ctx)
    ]

    second_gain_term = jnp.sum(grad_second * unit_second, axis=0)
    grad_residual = cotangent.astype(WIDE) + norm_back(residual, grad_second * gain_second)
    grad_branch = grad_residual.astype(LOW)
    grad_attended = after(dot(grad_branch, output_full, NT).astype(LOW), feed_part)
    down_came = None
    for step in range(1, n_ctx - 1):
        if step > 1:
            down_sent = line_step(down_slots, n_ctx, step, down_came)
            grad_attended = after(grad_attended, *down_sent)
        down_came = line_send(down_sent, n_ctx, step)
    grad_query, key_part, value_part = attend_back(
        query, cosine, sine, pair_all, bias, grad_attended, attended, log_total
    )
    pair_part = jnp.concatenate([key_part, value_part], 1)
    pair_part = jnp.concatenate([key_part, value_part], 1)
    if down_came is not None:
        down_came = tuple(after(values, grad_query) for values in down_came)
        down_sent = line_step(down_slots, n_ctx, n_ctx - 1, down_came)
    pair_part = after(pair_part, *down_sent)
    pair_slots = in_slots(pair_part)
    came, steps = None, []
    for step in range(1, n_ctx):
        sent = pair_slots[n_ctx - step]
        if came is not None:
            sent = (sent.astype(WIDE) + came.astype(WIDE)).astype(LOW)
        steps.append(sent)
        came = shift(sent, n_ctx, -1, range(n_ctx - step, n_ctx))
    pair_grad = pair_slots[0].astype(WIDE) + came.astype(WIDE)
    _, branch_summed = group_terms(
        [[attended], [first_hidden]],
        [[after(grad_branch, steps[min(1, n_ctx - 2)])], [grad_query]],
        [0, 1],
    )
    branch_terms = branch_summed([steps[-1]])
    grad_pair = turn_pair(after(pair_grad, grad_slots[1]), cosine, -sine)
    grad_first = dot(grad_query, query_full, NT) + dot(grad_pair, pair_weight, NT)
    first_gain_term = jnp.sum(grad_first * unit_first, axis=0)
    input_grad = (grad_residual + norm_back(tokens_wide, grad_first * gain_first)).astype(LOW)

    def ctx_rows_scatter(values, *earlier):
        parts = values.reshape(n_ctx, -1, values.shape[1])
        own = pick(parts, me, 0)
        came = [rotate(pick(parts, lax.rem(me + r, n_ctx), 0), n_ctx, r) for r in range(1, n_ctx)]
        return [own] + [after(values, *earlier) for values in came]

    branch_part = chip_scatter(branch_terms)
    gain_terms = jnp.pad(
        jnp.stack([first_gain_term, second_gain_term], 1), ((0, 0), (0, LANES - 2))
    ).astype(LOW)
    gain_parts = gain_terms.reshape(lax.axis_size(CHIPS), lax.axis_size("core"), -1, LANES)
    gain_part = pick(gain_parts, lax.axis_index("core"), 1)
    if lax.axis_size("core") == 2:
        gain_came = lax.ppermute(pick(gain_parts, 1 - lax.axis_index("core"), 1), "core", SWAP)
        gain_part = (gain_part.astype(WIDE) + gain_came.astype(WIDE)).astype(LOW)
    pair_terms = jnp.concatenate(
        [core_summed(first_hidden, grad_pair), gain_part.reshape(-1, LANES)], 1
    )
    pair_sum, middle = chip_scatter_steps(pair_terms, *grad_slots[1:])
    branch_part = after(branch_part, middle, *grad_slots[1:]).reshape(2, n_ctx, rows, width)
    branch_part = branch_part.transpose(1, 0, 2, 3).reshape(n_ctx * 2 * rows, width)
    total = lambda parts: sum(part.astype(WIDE) for part in parts)
    arrived = ctx_rows_scatter(branch_part, pair_sum)
    grad_slots[0] = after(grad_slots[0], arrived[1])
    if hidden_rows % LANES == 0:
        gate_weight_grad, up_weight_grad = (
            spread(grad_slots, me, kind, rows, n_dp) for kind in range(2)
        )
    else:
        both_grad = in_order(grad_slots, n_ctx, me).reshape(n_ctx, 2, rows, n_dp, hidden_rows)
        both_grad = both_grad.transpose(1, 2, 3, 0, 4).reshape(2, rows, hidden_units)
        gate_weight_grad, up_weight_grad = both_grad[0].astype(WIDE), both_grad[1].astype(WIDE)
    pair_weight_grad = total(ctx_rows_scatter(pair_sum, gate_weight_grad, up_weight_grad))
    arrived[2:] = [after(values, gate_weight_grad, up_weight_grad) for values in arrived[2:]]
    branch_grad = total(arrived).reshape(2, rows, width)
    down_sent = after(down_sent[0], pair_terms), down_sent[1]
    came = line_send(down_sent, n_ctx, n_ctx - 1)
    down_value = down_slots[0].astype(WIDE) + came[0].astype(WIDE) + came[1].astype(WIDE)
    block_output = (residual + down_value).astype(LOW)
    return (
        block_output,
        input_grad,
        pair_weight_grad[:, 2 * pair_width],
        pair_weight_grad[:, 2 * pair_width + 1],
        branch_grad[1],
        pair_weight_grad[:, :pair_width],
        pair_weight_grad[:, pair_width : 2 * pair_width],
        branch_grad[0],
        gate_weight_grad,
        up_weight_grad,
        down_weight_grad,
    )


def solution(mesh):
    n_dp, n_ctx = mesh.shape["dp"], mesh.shape["ctx"]
    n_core = 2 if n_dp % 2 == 0 else 1
    n_chips = n_dp // n_core
    n_y = math.isqrt(n_chips)
    while n_chips % n_y:
        n_y -= 1
    axes = ("y", "x", "core", "ctx")
    fine = Mesh(mesh.devices.reshape(n_y, n_chips // n_y, n_core, n_ctx), axes)
    matrix = P(axes, None)
    vector = P(axes)
    per_sequence = P(PLANES, None)
    return jax.shard_map(
        per_device,
        mesh=fine,
        in_specs=(matrix, matrix, per_sequence, per_sequence, vector, vector) + (matrix,) * 7,
        out_specs=(matrix, matrix, vector, vector) + (matrix,) * 7,
        check_vma=False,
    )
```

```python
import math

import jax
import jax.numpy as jnp
from jax import lax
from jax.experimental import pallas as pl
from jax.experimental.pallas import tpu as pltpu
from jax.sharding import Mesh
from jax.sharding import PartitionSpec as P

HEAD_DIM = 64
EPSILON = 1e-05
ROPE_BASE = 500000.0
MASKED_SCORE = -1e30
LANES = 128
GROUP = 4
SCORE_SCALE = HEAD_DIM**-0.5
KERNEL_MEMORY = 40 * 2**20
FEED_MEMORY = 56 * 2**20
FEED_STEP = 256
BACK_COST = pl.CostEstimate(flops=24_000_000_000, bytes_accessed=10_000_000, transcendentals=0)
COST = pl.CostEstimate(flops=1_000_000, bytes_accessed=1_000_000, transcendentals=0)

LOW = jnp.bfloat16
WIDE = jnp.float32
NN = (((1,), (0,)), ((), ()))
NT = (((1,), (1,)), ((), ()))
TN = (((0,), (0,)), ((), ()))


def dot(left, right, dims):
    return lax.dot_general(left, right, dims, preferred_element_type=WIDE)


def inverse_root(values):
    return lax.rsqrt(jnp.mean(values * values, axis=-1, keepdims=True) + EPSILON)


def norm_back(values, grad_normed):
    scaled = inverse_root(values)
    unit_rows = values * scaled
    return scaled * (
        grad_normed - unit_rows * jnp.mean(grad_normed * unit_rows, axis=-1, keepdims=True)
    )


def tie_kernel(*refs):
    del refs


def after(values, *earlier):
    anywhere = pl.BlockSpec(memory_space=pl.ANY)
    return pl.pallas_call(
        tie_kernel,
        in_specs=[anywhere] * (1 + len(earlier)),
        out_specs=anywhere,
        out_shape=jax.ShapeDtypeStruct(values.shape, values.dtype),
        input_output_aliases={0: 0},
        name="after",
    )(values, *earlier)


def turned(values, cosine, sine, first_half):
    ahead = pltpu.roll(values, LANES - HEAD_DIM // 2, 1)
    behind = pltpu.roll(values, HEAD_DIM // 2, 1)
    return values * cosine + jnp.where(first_half, ahead, behind) * sine


def lane_index():
    return lax.broadcasted_iota(jnp.int32, (1, LANES), 1)


def first_half_lanes():
    return lax.rem(lane_index(), HEAD_DIM) < HEAD_DIM // 2


def placed(block, member, head):
    start = member * GROUP * HEAD_DIM + (head // 2) * LANES
    values = block[:, start : start + LANES]
    if head % 2 != member:
        values = pltpu.roll(values, HEAD_DIM, 1)
    own = (lane_index() >= HEAD_DIM) if member else (lane_index() < HEAD_DIM)
    return jnp.where(own, values, jnp.zeros_like(values))


def forward_kernel(
    raw_ref, cos_ref, sin_ref, key_ref, value_ref, bias_ref, query_ref, out_ref, log_ref
):
    half = first_half_lanes()
    cosine, sine = cos_ref[...], sin_ref[...]
    wide = raw_ref.shape[1]
    block = jnp.concatenate(
        [
            turned(raw_ref[:, c : c + LANES], cosine, sine, half).astype(LOW).astype(WIDE)
            * SCORE_SCALE
            for c in range(0, wide, LANES)
        ],
        1,
    )
    query_ref[...] = block.astype(LOW)
    keys, values = key_ref[...], value_ref[...]
    span = GROUP * HEAD_DIM
    for member in range(2):
        parts = []
        for head in range(GROUP):
            query = placed(block, member, head).astype(LOW)
            scores = dot(keys, query, NT) + bias_ref[...]
            top = jnp.max(scores, 0, keepdims=True)
            exponent = jnp.exp(scores - top)
            total = jnp.sum(exponent, 0, keepdims=True)
            mixed = dot(values, exponent.astype(LOW), TN)
            parts.append(mixed[member * HEAD_DIM : (member + 1) * HEAD_DIM] / total)
            row = member * GROUP + head
            log_ref[row : row + 1, :] = top + jnp.log(total)
        out_ref[:, member * span : (member + 1) * span] = jnp.concatenate(parts, 0).T.astype(LOW)


def backward_kernel(
    query_ref,
    cos_ref,
    sin_ref,
    key_ref,
    value_ref,
    bias_ref,
    grad_ref,
    out_ref,
    log_ref,
    grad_query_ref,
    grad_key_ref,
    grad_value_ref,
):
    half = first_half_lanes()
    cosine, sine = cos_ref[...], -sin_ref[...]
    block = query_ref[...].astype(WIDE)
    grad = grad_ref[...].astype(WIDE)
    product = grad * out_ref[...].astype(WIDE)
    keys, values = key_ref[...], value_ref[...]
    span = GROUP * HEAD_DIM
    grad_keys = grad_values = None
    for member in range(2):
        parts = []
        product_t = product[:, member * span : (member + 1) * span].T
        for head in range(GROUP):
            query = placed(block, member, head).astype(LOW)
            grad_out = placed(grad, member, head).astype(LOW)
            row = member * GROUP + head
            delta = jnp.sum(
                product_t[head * HEAD_DIM : (head + 1) * HEAD_DIM], 0, keepdims=True
            )
            scores = dot(keys, query, NT) + bias_ref[...]
            probs = jnp.exp(scores - log_ref[row : row + 1, :])
            grad_probs = dot(values, grad_out, NT)
            grad_scores = (probs * (grad_probs - delta)).astype(LOW)
            key_part = dot(grad_scores, query, NN)
            value_part = dot(probs.astype(LOW), grad_out, NN)
            grad_keys = key_part if grad_keys is None else grad_keys + key_part
            grad_values = value_part if grad_values is None else grad_values + value_part
            query_part = dot(keys, grad_scores, TN)
            parts.append(query_part[member * HEAD_DIM : (member + 1) * HEAD_DIM] * SCORE_SCALE)
        grad_query = jnp.concatenate(parts, 0).T
        for c in range(0, span, LANES):
            grad_query_ref[:, member * span + c : member * span + c + LANES] = turned(
                grad_query[:, c : c + LANES], cosine, sine, half
            ).astype(LOW)
    grad_key_ref[...] = grad_keys.astype(LOW)
    grad_value_ref[...] = grad_values.astype(LOW)


def turn_kernel(values_ref, cos_ref, sin_ref, out_ref):
    half = first_half_lanes()
    width = values_ref.shape[1]
    for c in range(0, width // 2, LANES):
        out_ref[:, c : c + LANES] = turned(
            values_ref[:, c : c + LANES], cos_ref[...], sin_ref[...], half
        ).astype(LOW)
    out_ref[:, width // 2 :] = values_ref[:, width // 2 :].astype(LOW)


def feed_kernel(
    token_ref, goal_ref, gate_ref, up_ref, down_ref, active_ref, grad_gate_ref, grad_up_ref
):
    gate, up = dot(token_ref[...], gate_ref[...], NN), dot(token_ref[...], up_ref[...], NN)
    grad_active = dot(goal_ref[...], down_ref[...], NT)
    sigmoid = 1.0 / (1.0 + jnp.exp(-gate))
    silu = gate * sigmoid
    active_ref[...] = (silu * up).astype(LOW)
    grad_gate_ref[...] = (grad_active * up * sigmoid * (1.0 + gate * (1.0 - sigmoid))).astype(LOW)
    grad_up_ref[...] = (grad_active * silu).astype(LOW)


def second_kernel(grad_gate_ref, grad_up_ref, gate_ref, up_ref, out_ref):
    out_ref[...] = (
        dot(grad_gate_ref[...], gate_ref[...], NT) + dot(grad_up_ref[...], up_ref[...], NT)
    ).astype(LOW)


def feed_specs(count, width):
    whole = pl.BlockSpec((count, width), lambda i: (0, 0))
    return whole, pl.BlockSpec((count, FEED_STEP), lambda i: (0, i))


def feed(tokens, goal, both, down):
    count, width = tokens.shape
    hidden = down.shape[0]
    steps = hidden // FEED_STEP
    whole, part = feed_specs(count, width)
    return pl.pallas_call(
        feed_kernel,
        grid=(steps,),
        in_specs=[
            whole,
            whole,
            pl.BlockSpec((width, FEED_STEP), lambda i: (0, i)),
            pl.BlockSpec((width, FEED_STEP), lambda i: (0, i + steps)),
            pl.BlockSpec((FEED_STEP, width), lambda i: (i, 0)),
        ],
        out_specs=[part, part, part],
        out_shape=[jax.ShapeDtypeStruct((count, hidden), LOW)] * 3,
        compiler_params=pltpu.CompilerParams(vmem_limit_bytes=FEED_MEMORY),
        cost_estimate=COST,
        name="feed",
    )(tokens, goal, both, both, down)


def feed_back(grad_gate, grad_up, both):
    count, hidden = grad_gate.shape
    width = both.shape[0]
    whole, part = feed_specs(count, hidden)
    return pl.pallas_call(
        second_kernel,
        grid=(width // FEED_STEP,),
        in_specs=[
            whole,
            whole,
            pl.BlockSpec((FEED_STEP, hidden), lambda i: (i, 0)),
            pl.BlockSpec((FEED_STEP, hidden), lambda i: (i, 1)),
        ],
        out_specs=part,
        out_shape=jax.ShapeDtypeStruct((count, width), LOW),
        compiler_params=pltpu.CompilerParams(vmem_limit_bytes=FEED_MEMORY),
        cost_estimate=COST,
        name="feed_back",
    )(grad_gate, grad_up, both, both)


def weight_kernel(shared, parts, core_ref, *refs):
    del core_ref
    sides = max(shared) + 1
    lefts, rest = refs[: sides * parts], refs[sides * parts :]
    rights, out_ref = rest[: len(shared) * parts], rest[-1]
    came_ref = rest[-2] if len(rest) > len(shared) * parts + 1 else None
    for kind, side in enumerate(shared):

        @pl.when(pl.program_id(1) == kind)
        def _():
            total = None
            for part in range(parts):
                term = dot(
                    lefts[side * parts + part][...], rights[kind * parts + part][...], TN
                )
                total = term if total is None else total + term
            if came_ref is not None:
                total = total + came_ref[...].astype(WIDE)
            out_ref[...] = total.astype(LOW)


def weight_rows(lefts, rights, shared, index, chips, n_core, came=None):
    tokens, columns = rights[0][0].shape
    kinds, parts = len(rights), len(rights[0])
    size = lefts[0][0].shape[1] // (chips * n_core)
    left = pl.BlockSpec((tokens, size), lambda i, g, core: (0, i * n_core + core[0]))
    right = pl.BlockSpec((tokens, columns), lambda i, g, core: (0, 0))
    out = pl.BlockSpec((size, columns), lambda i, g, core: (i * kinds + g, 0))
    return pl.pallas_call(
        lambda *refs: weight_kernel(shared, parts, *refs),
        grid_spec=pltpu.PrefetchScalarGridSpec(
            num_scalar_prefetch=1,
            grid=(chips, kinds),
            in_specs=[left] * (parts * len(lefts))
            + [right] * (kinds * parts)
            + ([] if came is None else [out]),
            out_specs=out,
        ),
        out_shape=jax.ShapeDtypeStruct((chips * kinds * size, columns), LOW),
        compiler_params=pltpu.CompilerParams(vmem_limit_bytes=FEED_MEMORY),
        cost_estimate=pl.CostEstimate(
            flops=2 * chips * kinds * size * columns * tokens * parts,
            bytes_accessed=2 * chips * kinds * size * columns,
            transcendentals=0,
        ),
        name="weight_rows",
    )(
        jnp.reshape(index, (1,)).astype(jnp.int32),
        *(part for side in lefts for part in side),
        *(part for kind in rights for part in kind),
        *([] if came is None else [came]),
    )


def fixed_block(shape):
    return pl.BlockSpec(shape, lambda i: (0, 0))


def attention_blocks(count, length, steps):
    span = 2 * GROUP * HEAD_DIM
    return (
        pl.BlockSpec((count, span), lambda i: (0, i)),
        pl.BlockSpec((length, LANES), lambda i: (0, i)),
        pl.BlockSpec((length, LANES), lambda i: (0, i + steps)),
        pl.BlockSpec((2 * GROUP, count), lambda i: (i, 0)),
    )


def attend(raw, cosine, sine, pair, bias):
    count, length = raw.shape[0], pair.shape[0]
    steps = pair.shape[1] // 2 // LANES
    wide, key, value, rows = attention_blocks(count, length, steps)
    table = fixed_block((count, LANES))
    return pl.pallas_call(
        forward_kernel,
        grid=(steps,),
        in_specs=[wide, table, table, key, value, fixed_block((length, count))],
        out_specs=[wide, wide, rows],
        out_shape=[
            jax.ShapeDtypeStruct(raw.shape, LOW),
            jax.ShapeDtypeStruct(raw.shape, LOW),
            jax.ShapeDtypeStruct((steps * 2 * GROUP, count), WIDE),
        ],
        compiler_params=pltpu.CompilerParams(vmem_limit_bytes=KERNEL_MEMORY),
        cost_estimate=COST,
        name="attend",
    )(raw, cosine, sine, pair, pair, bias)


def attend_back(query, cosine, sine, pair, bias, grad, out, log_total):
    count, length = query.shape[0], pair.shape[0]
    steps = pair.shape[1] // 2 // LANES
    wide, key, value, rows = attention_blocks(count, length, steps)
    table = fixed_block((count, LANES))
    half = jax.ShapeDtypeStruct((length, steps * LANES), LOW)
    return pl.pallas_call(
        backward_kernel,
        grid=(steps,),
        in_specs=[wide, table, table, key, value, fixed_block((length, count)), wide, wide, rows],
        out_specs=[wide, key, key],
        out_shape=[jax.ShapeDtypeStruct(query.shape, LOW), half, half],
        compiler_params=pltpu.CompilerParams(vmem_limit_bytes=KERNEL_MEMORY),
        cost_estimate=BACK_COST,
        name="attend_back",
    )(query, cosine, sine, pair, pair, bias, grad, out, log_total)


def turn_pair(values, cosine, sine):
    return pl.pallas_call(
        turn_kernel, out_shape=jax.ShapeDtypeStruct(values.shape, LOW), name="turn_pair"
    )(values, cosine, sine)


def spread_kernel(me_ref, *refs):
    count, out_ref = len(refs) - 1, refs[-1]
    width = refs[0].shape[1]
    for r in range(count):
        place = lax.rem(me_ref[0] - r + count, count)
        start = pl.multiple_of(place * width, LANES)
        out_ref[:, pl.ds(start, width)] = refs[r][...].astype(WIDE)


def spread(slots, me, kind, rows, blocks):
    count, width = len(slots), slots[0].shape[1] // blocks
    part = pl.BlockSpec((rows, width), lambda i, me: (kind, i))
    return pl.pallas_call(
        spread_kernel,
        grid_spec=pltpu.PrefetchScalarGridSpec(
            num_scalar_prefetch=1,
            grid=(blocks,),
            in_specs=[part] * count,
            out_specs=pl.BlockSpec((rows, count * width), lambda i, me: (0, i)),
        ),
        out_shape=jax.ShapeDtypeStruct((rows, blocks * count * width), WIDE),
        name="spread",
    )(jnp.reshape(me, (1,)).astype(jnp.int32), *slots)


def shift(values, count, step, senders):
    pairs = [(i, i + step) for i in senders if 0 <= i + step < count]
    return lax.ppermute(values, "ctx", pairs)


def rotate(values, count, step):
    return lax.ppermute(values, "ctx", [(i, (i + step) % count) for i in range(count)])


def line_slot(up, down, count, me, r):
    return up[0] if r == 0 else jnp.where(me >= r, up[r], down[count - r])


def line_chains(own, count):
    up, down = [own], [own]
    for s in range(1, count):
        up.append(shift(up[-1], count, 1, range(s - 1, count)))
        down.append(shift(down[-1], count, -1, range(0, count - s + 1)))
    return up, down


def line_groups(count):
    first = [r for r in range(count) if r == 0 or max(r, count - r) < count - 1]
    groups = [first, [r for r in range(count) if r not in first]]
    return [group for group in groups if group]


def line_step(slots, count, step, came):
    up, down = slots[step], slots[count - step]
    if came is not None:
        up = (up.astype(WIDE) + came[0].astype(WIDE)).astype(LOW)
        down = (down.astype(WIDE) + came[1].astype(WIDE)).astype(LOW)
    return up, down


def line_send(pair, count, step):
    up = shift(pair[0], count, 1, range(0, step))
    return up, shift(pair[1], count, -1, range(count - step, count))


def line_gather_up(own, count):
    return [own] + [shift(own, count, s, range(count)) for s in range(1, count)]


def in_order(slots, count, me):
    out = jnp.zeros((count, *slots[0].shape), slots[0].dtype)
    for r in range(count):
        out = lax.dynamic_update_index_in_dim(out, slots[r], lax.rem(me - r + count, count), 0)
    return out


CHIPS = ("y", "x")
PLANES = ("y", "x", "core")
SWAP = [(0, 1), (1, 0)]


def pick(values, index, axis):
    return lax.dynamic_index_in_dim(values, index, axis, keepdims=False)


def small_square():
    return lax.axis_size("y") == 2 and lax.axis_size("x") == 2 and lax.axis_size("core") == 2


def plane_gather(values):
    return lax.all_gather(values, PLANES, axis=0, tiled=True)


def core_columns(values, index):
    n_core, chips = lax.axis_size("core"), lax.axis_size(CHIPS)
    size = values.shape[1] // (chips * n_core)
    return jnp.concatenate(
        [
            lax.dynamic_slice_in_dim(values, (chip * n_core + index) * size, size, 1)
            for chip in range(chips)
        ],
        1,
    )


def core_term(left, right):
    if lax.axis_size("core") == 1:
        return None
    return dot(core_columns(left, 1 - lax.axis_index("core")), right, TN).astype(LOW)


def core_summed(left, right, sent=None):
    if lax.axis_size("core") == 1:
        return dot(left, right, TN).astype(LOW)
    sent = core_term(left, right) if sent is None else sent
    came = lax.ppermute(sent, "core", SWAP)
    own = core_columns(left, lax.axis_index("core"))
    return (dot(own, right, TN) + came.astype(WIDE)).astype(LOW)


def group_terms(lefts, rights, shared):
    n_core, chips = lax.axis_size("core"), lax.axis_size(CHIPS)
    core = lax.axis_index("core")
    size = lefts[0][0].shape[1] // (chips * n_core)
    if n_core == 2 and size % LANES == 0:
        sent = weight_rows(lefts, rights, shared, 1 - core, chips, n_core)

        def summed(tied, last=()):
            came = lax.ppermute(after(sent, *tied), "core", SWAP)
            came = after(came, *last) if last else came
            return weight_rows(lefts, rights, shared, core, chips, n_core, came)

        return sent, summed
    each = [
        core_summed(jnp.concatenate(lefts[side], 0), jnp.concatenate(kind, 0))
        for kind, side in zip(rights, shared)
    ]
    each = jnp.concatenate([values.reshape(chips, 1, size, -1) for values in each], 1)
    each = each.reshape(chips * len(rights) * size, -1)
    return each, lambda tied, last=(): each


def chip_scatter(values):
    return lax.psum_scatter(values, CHIPS, scatter_dimension=0, tiled=True)


def chip_scatter_steps(values, *between):
    if not small_square():
        return chip_scatter(values), values
    columns = values.shape[1]
    y, x = lax.axis_index("y"), lax.axis_index("x")
    parts = values.reshape(2, 2, -1, columns)
    half = parts.shape[2] // 2
    add = lambda a, b: (a.astype(WIDE) + b.astype(WIDE)).astype(LOW)
    top, bottom = parts[:, :, :half], parts[:, :, half:]
    top_came = lax.ppermute(pick(top, 1 - x, 1), "x", SWAP)
    bottom_came = lax.ppermute(pick(bottom, 1 - y, 0), "y", SWAP)
    top = after(add(pick(top, x, 1), top_came), *between)
    bottom = add(pick(bottom, y, 0), bottom_came)
    middle = pick(bottom, 1 - x, 0)
    top_came = lax.ppermute(pick(top, 1 - y, 0), "y", SWAP)
    bottom_came = lax.ppermute(middle, "x", SWAP)
    top = add(pick(top, y, 0), top_came)
    bottom = add(pick(bottom, x, 0), bottom_came)
    return jnp.concatenate([top, bottom], 0), middle


def per_device(
    inputs,
    cotangent,
    segment_ids,
    real_entry_flags,
    attention_gain,
    feedforward_gain,
    query_weight,
    key_weight,
    value_weight,
    output_weight,
    gate_weight,
    up_weight,
    down_weight,
):
    n_ctx = lax.axis_size("ctx")
    n_dp = lax.axis_size(PLANES)
    me = lax.axis_index("ctx")
    entry_count, width = inputs.shape
    query_width = query_weight.shape[1]
    pair_width = key_weight.shape[1]
    hidden_units = gate_weight.shape[1]
    rows = gate_weight.shape[0]
    hidden_rows = down_weight.shape[0]
    hidden_chunk = hidden_units // n_ctx

    def ctx_rows_gather(values):
        slots = [values] + [rotate(values, n_ctx, r) for r in range(1, n_ctx)]
        return in_order(slots, n_ctx, me).reshape(n_ctx * rows, -1)

    gains = jnp.pad(
        jnp.stack([attention_gain, feedforward_gain], 1), ((0, 0), (0, LANES - 2))
    )
    pair_low = jnp.concatenate([key_weight, value_weight, gains], 1).astype(LOW)
    pair_rows = ctx_rows_gather(pair_low)
    pair_full = plane_gather(pair_rows)

    branch_low = jnp.concatenate([query_weight, output_weight], 1).astype(LOW)
    branch_rows = ctx_rows_gather(after(branch_low, pair_rows))
    branch_full = plane_gather(branch_rows)

    both = jnp.stack([gate_weight, up_weight], 1).astype(LOW)
    both = both.reshape(rows, 2, n_dp, n_ctx, hidden_rows)
    chunk_for = lambda place: pick(both, place, 3).reshape(rows, 2 * hidden_chunk)

    gain_first = pair_full[:, 2 * pair_width].astype(WIDE)
    gain_second = pair_full[:, 2 * pair_width + 1].astype(WIDE)
    pair_weight = pair_full[:, : 2 * pair_width]
    query_full = branch_full[:, :query_width]
    output_full = branch_full[:, query_width:]

    spans = segment_ids[0]
    reality = real_entry_flags[0]
    opening = me * entry_count
    places = opening + jnp.arange(entry_count, dtype=jnp.int32)
    own_spans = lax.dynamic_slice_in_dim(spans, opening, entry_count)
    doc_starts = jnp.sum((spans[None, :] < own_spans[:, None]).astype(jnp.int32), axis=1)
    offsets = (places - doc_starts).astype(WIDE)
    frequency = ROPE_BASE ** (
        -(jnp.arange(HEAD_DIM // 2, dtype=WIDE) * 2.0 / HEAD_DIM)
    )
    angle = offsets[:, None] * frequency[None, :]
    cosine, sine = jnp.cos(angle), jnp.sin(angle)
    cosine = jnp.concatenate([cosine] * 4, 1)
    sine = jnp.concatenate([-sine, sine] * 2, 1)
    key_places, key_spans, key_reality = [], [], []
    for r in range(n_ctx):
        start = (me - r) * entry_count
        key_places.append(start + jnp.arange(entry_count, dtype=jnp.int32))
        start = jnp.maximum(start, 0)
        key_spans.append(lax.dynamic_slice_in_dim(spans, start, entry_count))
        key_reality.append(lax.dynamic_slice_in_dim(reality, start, entry_count))
    key_places = jnp.concatenate(key_places)[:, None]
    key_spans = jnp.concatenate(key_spans)[:, None]
    key_reality = jnp.concatenate(key_reality)[:, None]
    allowed = (
        (own_spans[None, :] == key_spans)
        & (key_places <= places[None, :])
        & (key_places >= 0)
        & (key_reality == 1)
    ) | (key_places == places[None, :])
    bias = jnp.where(allowed, 0.0, MASKED_SCORE).astype(WIDE)

    tokens_wide = inputs.astype(WIDE)
    unit_first = tokens_wide * inverse_root(tokens_wide)
    first_hidden = (unit_first * gain_first).astype(LOW)
    both_slots = [chunk_for(me)] + [
        rotate(after(chunk_for(lax.rem(me + r, n_ctx)), branch_rows), n_ctx, r)
        for r in range(1, n_ctx)
    ]
    both_rows = in_order(both_slots, n_ctx, me).reshape(n_ctx * rows, 2 * hidden_chunk)
    both_full = plane_gather(both_rows)
    down_full = plane_gather(after(down_weight.astype(LOW), branch_rows))
    pair_own = turn_pair(dot(first_hidden, pair_weight, NN), cosine, sine)
    pair_all = jnp.concatenate(line_gather_up(after(pair_own, both_rows), n_ctx), 0)
    cot_sent = after(cotangent, pair_all)
    cot_slots = [cotangent] + [rotate(cot_sent, n_ctx, r) for r in range(1, n_ctx)]
    raw_query = dot(first_hidden, query_full, NN)
    query, attended, log_total = attend(raw_query, cosine, sine, pair_all, bias)

    residual = tokens_wide + dot(attended, output_full, NN)
    unit_second = residual * inverse_root(residual)
    second_hidden = (unit_second * gain_second).astype(LOW)
    up_chain, down_chain = line_chains(after(second_hidden, *cot_slots[1:]), n_ctx)
    groups = line_groups(n_ctx)
    hidden, cot, active, gates, ups = [], [], [], [], []
    second_slots, down_slots = [None] * n_ctx, [None] * n_ctx
    for group in groups:
        tokens = jnp.concatenate(
            [line_slot(up_chain, down_chain, n_ctx, me, r) for r in group], 0
        )
        goal = jnp.concatenate([cot_slots[r] for r in group], 0)
        if active:
            goal = after(goal, active[-1])
        group_active, grad_gate, grad_up = feed(tokens, goal, both_full, down_full)
        for kept, value in zip(
            (hidden, cot, active, gates, ups), (tokens, goal, group_active, grad_gate, grad_up)
        ):
            kept.append(value)

    second = ()
    for k in reversed(range(len(groups))):
        if k < len(groups) - 1:
            ups[k] = after(ups[k], second)
        second = feed_back(gates[k], ups[k], both_full)
        for i, r in enumerate(groups[k]):
            second_slots[r] = second[i * entry_count : (i + 1) * entry_count]

    def down_terms(k, *tied):
        if tied:
            active[k] = after(active[k], *tied)
        down_out = dot(active[k], down_full, NN).astype(LOW)
        for i, r in enumerate(groups[k]):
            down_slots[r] = down_out[i * entry_count : (i + 1) * entry_count]
        return down_out

    first = line_step(second_slots, n_ctx, 1, None)
    came, steps = line_send(first, n_ctx, 1), [first]
    early = down_terms(-1, *first)
    for step in range(2, n_ctx):
        sent = line_step(second_slots, n_ctx, step, came)
        if step == 2:
            sent = after(sent[0], early), sent[1]
        steps.append(sent)
        came = line_send(sent, n_ctx, step)
    gates[0] = after(gates[0], *steps[min(1, n_ctx - 2)])
    feed_sent, feed_summed = group_terms([hidden, active], [gates, ups, cot], [0, 0, 1])
    if len(groups) > 1:
        late = down_terms(0)
        came = after(came[0], late), came[1]
    grad_second = second_slots[0].astype(WIDE) + came[0].astype(WIDE) + came[1].astype(WIDE)
    down_sent = tuple(
        after(values, grad_second) for values in line_step(down_slots, n_ctx, 1, None)
    )
    feed_part = feed_summed(steps[-1], came)
    in_slots = lambda values: [
        values[r * entry_count : (r + 1) * entry_count] for r in range(n_ctx)
    ]
    feed_rows = chip_scatter(feed_part).reshape(3, n_ctx * rows, hidden_chunk)
    both_grad_rows = feed_rows[:2]
    down_weight_grad = feed_rows[2].astype(WIDE)

    both_grad_parts = both_grad_rows.reshape(2, n_ctx, rows, hidden_chunk)
    part_for = lambda place: pick(both_grad_parts, place, 1).reshape(2 * rows, hidden_chunk)
    grad_slots = [part_for(me)] + [
        rotate(part_for(lax.rem(me + r, n_ctx)), n_ctx, r) for r in range(1, n_ctx)
    ]

    second_gain_term = jnp.sum(grad_second * unit_second, axis=0)
    grad_residual = cotangent.astype(WIDE) + norm_back(residual, grad_second * gain_second)
    grad_branch = grad_residual.astype(LOW)
    grad_attended = after(dot(grad_branch, output_full, NT).astype(LOW), feed_part)
    down_came = None
    for step in range(1, n_ctx - 1):
        if step > 1:
            down_sent = line_step(down_slots, n_ctx, step, down_came)
            grad_attended = after(grad_attended, *down_sent)
        down_came = line_send(down_sent, n_ctx, step)
    grad_query, key_part, value_part = attend_back(
        query, cosine, sine, pair_all, bias, grad_attended, attended, log_total
    )
    pair_part = jnp.concatenate([key_part, value_part], 1)
    pair_part = jnp.concatenate([key_part, value_part], 1)
    if down_came is not None:
        down_came = tuple(after(values, grad_query) for values in down_came)
        down_sent = line_step(down_slots, n_ctx, n_ctx - 1, down_came)
    pair_part = after(pair_part, *down_sent)
    pair_slots = in_slots(pair_part)
    came, steps = None, []
    for step in range(1, n_ctx):
        sent = pair_slots[n_ctx - step]
        if came is not None:
            sent = (sent.astype(WIDE) + came.astype(WIDE)).astype(LOW)
        steps.append(sent)
        came = shift(sent, n_ctx, -1, range(n_ctx - step, n_ctx))
    pair_grad = pair_slots[0].astype(WIDE) + came.astype(WIDE)
    _, branch_summed = group_terms(
        [[attended], [first_hidden]],
        [[after(grad_branch, steps[min(1, n_ctx - 2)])], [grad_query]],
        [0, 1],
    )
    branch_terms = branch_summed([steps[-1]])
    grad_pair = turn_pair(pair_grad, cosine, -sine)
    grad_first = dot(grad_query, query_full, NT) + dot(grad_pair, pair_weight, NT)
    first_gain_term = jnp.sum(grad_first * unit_first, axis=0)
    input_grad = (grad_residual + norm_back(tokens_wide, grad_first * gain_first)).astype(LOW)

    def ctx_rows_scatter(values, *earlier):
        parts = values.reshape(n_ctx, -1, values.shape[1])
        own = pick(parts, me, 0)
        came = [rotate(pick(parts, lax.rem(me + r, n_ctx), 0), n_ctx, r) for r in range(1, n_ctx)]
        return [own] + [after(values, *earlier) for values in came]

    branch_part = chip_scatter(branch_terms)
    gain_terms = jnp.pad(
        jnp.stack([first_gain_term, second_gain_term], 1), ((0, 0), (0, LANES - 2))
    ).astype(LOW)
    gain_parts = gain_terms.reshape(lax.axis_size(CHIPS), lax.axis_size("core"), -1, LANES)
    gain_part = pick(gain_parts, lax.axis_index("core"), 1)
    if lax.axis_size("core") == 2:
        gain_came = lax.ppermute(pick(gain_parts, 1 - lax.axis_index("core"), 1), "core", SWAP)
        gain_part = (gain_part.astype(WIDE) + gain_came.astype(WIDE)).astype(LOW)
    pair_terms = jnp.concatenate(
        [core_summed(first_hidden, grad_pair), gain_part.reshape(-1, LANES)], 1
    )
    pair_sum, middle = chip_scatter_steps(pair_terms, *grad_slots[1:])
    branch_part = after(branch_part, middle, *grad_slots[1:]).reshape(2, n_ctx, rows, width)
    branch_part = branch_part.transpose(1, 0, 2, 3).reshape(n_ctx * 2 * rows, width)
    total = lambda parts: sum(part.astype(WIDE) for part in parts)
    arrived = ctx_rows_scatter(branch_part, pair_sum)
    grad_slots[0] = after(grad_slots[0], arrived[1])
    if hidden_rows % LANES == 0:
        gate_weight_grad, up_weight_grad = (
            spread(grad_slots, me, kind, rows, n_dp) for kind in range(2)
        )
    else:
        both_grad = in_order(grad_slots, n_ctx, me).reshape(n_ctx, 2, rows, n_dp, hidden_rows)
        both_grad = both_grad.transpose(1, 2, 3, 0, 4).reshape(2, rows, hidden_units)
        gate_weight_grad, up_weight_grad = both_grad[0].astype(WIDE), both_grad[1].astype(WIDE)
    pair_weight_grad = total(ctx_rows_scatter(pair_sum, gate_weight_grad, up_weight_grad))
    arrived[2:] = [after(values, gate_weight_grad, up_weight_grad) for values in arrived[2:]]
    branch_grad = total(arrived).reshape(2, rows, width)
    down_sent = after(down_sent[0], pair_terms), down_sent[1]
    came = line_send(down_sent, n_ctx, n_ctx - 1)
    down_value = down_slots[0].astype(WIDE) + came[0].astype(WIDE) + came[1].astype(WIDE)
    block_output = (residual + down_value).astype(LOW)
    return (
        block_output,
        input_grad,
        pair_weight_grad[:, 2 * pair_width],
        pair_weight_grad[:, 2 * pair_width + 1],
        branch_grad[1],
        pair_weight_grad[:, :pair_width],
        pair_weight_grad[:, pair_width : 2 * pair_width],
        branch_grad[0],
        gate_weight_grad,
        up_weight_grad,
        down_weight_grad,
    )


def solution(mesh):
    n_dp, n_ctx = mesh.shape["dp"], mesh.shape["ctx"]
    n_core = 2 if n_dp % 2 == 0 else 1
    n_chips = n_dp // n_core
    n_y = math.isqrt(n_chips)
    while n_chips % n_y:
        n_y -= 1
    axes = ("y", "x", "core", "ctx")
    fine = Mesh(mesh.devices.reshape(n_y, n_chips // n_y, n_core, n_ctx), axes)
    matrix = P(axes, None)
    vector = P(axes)
    per_sequence = P(PLANES, None)
    return jax.shard_map(
        per_device,
        mesh=fine,
        in_specs=(matrix, matrix, per_sequence, per_sequence, vector, vector) + (matrix,) * 7,
        out_specs=(matrix, matrix, vector, vector) + (matrix,) * 7,
        check_vma=False,
    )
```
